1024 devices in a mesh: dp: 16 (over z), expert: 16 (over y, core), tensor: 4 (over x).
Axes of the slice: x: 4, y: 8, z: 16, core: 2. Of those that a mesh axis runs over, the one named last changes fastest.
Arguments:
- grad_out: bfloat16 [32768, 1792], P(('dp', 'expert')), may hold values from -6 to 6
- expert_ids: int32 [32768, 8], P(('dp', 'expert')), may hold values from 0 to 63, all different within a row; in each aligned block of 32 rows (0 to 31, 32 to 63, ...) at most 6 rows name the same one
- gate_probs: float32 [32768, 8], P(('dp', 'expert')), may hold values from 0.1 to 0.6
- saved_inputs: bfloat16 [16, 16, 4, 16, 6, 1792], P('dp', 'expert'), may hold values from -6 to 6
- w_gate: bfloat16 [16, 1792, 1280], P('expert', None, 'tensor'), may hold values from -0.125 to 0.125
- w_up: bfloat16 [16, 1792, 1280], P('expert', None, 'tensor'), may hold values from -0.125 to 0.125
- w_down: bfloat16 [16, 1792, 1280], P('expert', None, 'tensor'), may hold values from -0.15625 to 0.15625
Outputs:
- input_grad: bfloat16 [32768, 1792], P(('dp', 'expert'))
- prob_grad: float32 [32768, 8], P(('dp', 'expert'))
- gate_weight_grad: float32 [16, 1792, 1280], P('expert', 'dp', 'tensor')
- up_weight_grad: float32 [16, 1792, 1280], P('expert', 'dp', 'tensor')
- down_weight_grad: float32 [16, 1792, 1280], P('expert', 'dp', 'tensor')
The draws below stay inside these ranges and needn't reach their ends.
Inputs may be any that keep to these rules, and one draw needn't show every extreme that they name: `expert_ids`: each row names 8 different experts; in every aligned block of 32 rows no expert is named by more than 6 rows.
All inputs are finite; a program needn't handle non-finite values.
Results may differ from the reference program's by a relative error of at most 0.02.
Values may be sent and summed in bfloat16 or wider, within the bound.
A program may use at most 64 MiB of HBM per device.

```python
import math
import jax
import jax.numpy as jnp
import numpy as np
from jax import lax

D = 1792
FF = 1280
TOP = 8
EXP_DEV = 4
TOK_DEV = 128
EXPERTS = 64
CAP = 6
TOKENS = 32768
N_DP = 16
N_EXPERT = 16
N_TENSOR = 4


def with_spikes(array, rng, source, target, parts, factor):
    owner, partner = [(jnp.arange(array.shape[dim]) // (array.shape[dim] // parts)).reshape([-1 if axis == dim else 1 for axis in range(array.ndim)]) for dim in (source, target)]
    chosen = jax.random.permutation(rng, parts)[partner]
    strong = (owner == chosen) | (owner == (partner + parts // 2) % parts)
    return jnp.where(strong, factor * array, array)


def block_scale(stream_key, extent, pieces, least, high):
    def one(position, parts):
        heights = jax.random.uniform(jax.random.fold_in(jax.random.fold_in(stream_key, 6), position), (parts,), jnp.float32, least / len(pieces), high / len(pieces))
        return jnp.repeat(jnp.exp(heights), extent[position] // parts).reshape((-1,) + (1,) * (len(extent) - position - 1))

    gain = one(*pieces[0])
    for cut in pieces[1:]:
        gain = gain * one(*cut)
    return gain


def deal_out(rng, own, number, rows, amount, top, reach, slope):
    ranking = jax.random.permutation(rng, amount)
    crowded, ordinary = portions_of(amount, rows * top, reach, slope, True), portions_of(amount, rows * top, reach, slope, False)
    places = jnp.arange(amount)

    def named(lengths, offset_by):
        used = int((lengths > 0).sum())
        fixed = max(1, used // 4)
        passed = fixed + (places - fixed + offset_by * (used - fixed)) % max(1, amount - fixed)
        return jnp.zeros((amount,), jnp.int32).at[ranking[jnp.where(places < fixed, places, passed)]].set(jnp.asarray(lengths, jnp.int32))

    lengths = jnp.where(number % 4 == 0, named(crowded, number // 4), named(ordinary, number - number // 4 - 1))
    mixed = jax.random.permutation(jax.random.fold_in(own, 3), amount)
    giver, sink = mixed[0:amount // 2 * 2:2], mixed[1:amount // 2 * 2:2]
    room = jnp.minimum(lengths[giver] - 1, reach - lengths[sink]) // 2
    room = jnp.where((giver == ranking[0]) | (sink == ranking[0]) | (lengths[sink] == 0), 0, jnp.maximum(room, 0))
    passed = jax.random.randint(jax.random.fold_in(own, 4), (amount // 2,), 0, 1 << 20) % (room + 1)
    lengths = lengths.at[giver].add(-passed).at[sink].add(passed)
    members = jnp.searchsorted(jnp.cumsum(lengths), jnp.arange(rows * top), side="right").astype(jnp.int32)
    listing = members.reshape(top, rows).T
    listing = listing[jax.random.permutation(jax.random.fold_in(own, 1), rows)]
    offset_by = jax.random.randint(jax.random.fold_in(own, 2), (rows, 1), 0, top)
    return jnp.take_along_axis(listing, (jnp.arange(top)[None, :] + offset_by) % top, axis=1)


def portions_of(count, total, reach, slope, full):
    weights = [(1 << 20) // math.isqrt(standing ** slope) + 1 for standing in range(1, count + 1)]
    largest = reach if full else min(reach, max(-(-total // count), total * weights[0] // sum(weights)))
    least = 1 if total - largest >= count - 1 else 0
    given, rest = [largest] + [least] * (count - 1), total - largest - least * (count - 1)
    while rest > 0:
        candidates = [i for i in range(1, count) if given[i] < largest] or [i for i in range(1, count) if given[i] < reach]
        whole, budget = sum([weights[i] for i in candidates]), rest
        for i in candidates:
            extra = min(reach - given[i], max(1, budget * weights[i] // whole), rest)
            given[i] = given[i] + extra
            rest = rest - extra
    return np.array(given)


def normal_values(own_key, dims, scale, reach, shards=(), kind=jnp.bfloat16):
    result = scale * jax.random.normal(own_key, dims, jnp.float32)
    if shards:
        result = result * block_scale(own_key, dims, shards, -0.22, 0.18)
    return jnp.clip(result, -reach, reach).astype(kind)


def bell_draw_with(stream_key, shape, width, bound, split, heavy, kind=jnp.bfloat16):
    array = width * jax.random.normal(stream_key, shape, jnp.float32)
    if split:
        array = array * block_scale(stream_key, shape, split, -0.22, 0.18)
    return jnp.clip(with_spikes(array, jax.random.fold_in(stream_key, 3), *heavy), -bound, bound).astype(kind)


def setup_inputs(seed: int = 0) -> dict:
    keys = jax.random.split(jax.random.key(seed), 8)
    grad_out = normal_values(keys[0], (TOKENS, D), 1.0, 6.0, ((0, 256),))
    expert_ids_keys = jax.random.split(jax.random.fold_in(keys[1], 1), TOKENS // (TOK_DEV // N_TENSOR))
    expert_ids_turns = jax.random.permutation(jax.random.fold_in(keys[1], 3), TOKENS // (TOK_DEV // N_TENSOR))
    expert_ids = jax.vmap(lambda own, number: deal_out(jax.random.fold_in(keys[1], 2), own, number, TOK_DEV // N_TENSOR, EXPERTS, TOP, CAP, 2))(expert_ids_keys, expert_ids_turns).reshape((TOKENS, TOP))
    gate_probs = jnp.clip(0.1 + 0.5 * jax.random.uniform(keys[2], (TOKENS, TOP), jnp.float32) ** block_scale(keys[2], (TOKENS, TOP), ((0, 256),), -0.2, 0.2), 0.1, 0.6)
    saved_inputs = bell_draw_with(keys[3], (N_DP, N_EXPERT, N_TENSOR, N_EXPERT, CAP, D), 1.0, 6.0, ((0, 16), (1, 16)), (0, 5, 16, 2.0))
    w_gate = normal_values(keys[4], (N_EXPERT, D, FF), D ** -0.5, 0.125, ((0, 16), (2, 4)))
    w_up = normal_values(keys[5], (N_EXPERT, D, FF), D ** -0.5, 0.125, ((0, 16), (2, 4)))
    w_down = normal_values(keys[6], (N_EXPERT, D, FF), FF ** -0.5, 0.15625, ((0, 16), (2, 4)))
    return {"grad_out": grad_out, "expert_ids": expert_ids, "gate_probs": gate_probs, "saved_inputs": saved_inputs, "w_gate": w_gate, "w_up": w_up, "w_down": w_down}


def silu_parts(pre_gate):
    sigmoid_val = jax.nn.sigmoid(pre_gate)
    return pre_gate * sigmoid_val, sigmoid_val * (1.0 + pre_gate * (1.0 - sigmoid_val))


def to_bf16_back(values):
    return lax.optimization_barrier(values.astype(jnp.bfloat16)).astype(jnp.float32)


def reference(grad_out, expert_ids, gate_probs, saved_inputs, w_gate, w_up, w_down):
    share_rows = TOK_DEV // N_TENSOR
    per_expert = N_TENSOR * N_EXPERT * CAP
    total_slots = N_DP * N_EXPERT * per_expert
    hidden_dev = FF // N_TENSOR
    positions = jnp.arange(N_EXPERT, dtype=jnp.int32)
    onehot = (((expert_ids[:, :, None] // EXP_DEV) == positions) & ((expert_ids[:, :, None] % EXP_DEV) == 0)).astype(jnp.int32)
    routed = jnp.sum(onehot, axis=1)
    blocked = routed.reshape(-1, share_rows, N_EXPERT)
    slot_rank = (jnp.cumsum(blocked, axis=1) - blocked).reshape(TOKENS, N_EXPERT)
    token_ids = jnp.arange(TOKENS, dtype=jnp.int32)
    group_ids = token_ids // (N_EXPERT * TOK_DEV)
    source_pos = (token_ids // TOK_DEV) % N_EXPERT
    share_ids = (token_ids % TOK_DEV) // share_rows
    slot_index = (((group_ids[:, None] * N_EXPERT + positions[None, :]) * N_TENSOR + share_ids[:, None]) * N_EXPERT + source_pos[:, None]) * CAP + slot_rank
    slot_index = jnp.where(routed > 0, slot_index, total_slots).astype(jnp.int32)
    prob_tok = jnp.sum(onehot.astype(jnp.float32) * gate_probs[:, :, None], axis=1).astype(jnp.bfloat16)
    flat_index = slot_index.reshape(-1)
    slot_token = jnp.full((total_slots,), TOKENS, jnp.int32).at[flat_index].set(jnp.broadcast_to(token_ids[:, None], (TOKENS, N_EXPERT)).reshape(-1).astype(jnp.int32), mode="drop")
    slot_weight = jnp.zeros((total_slots,), jnp.bfloat16).at[flat_index].set(prob_tok.reshape(-1), mode="drop")
    padded_grad = jnp.concatenate([grad_out, jnp.zeros((1, D), grad_out.dtype)], axis=0)
    slot_grad = padded_grad[slot_token]
    gate_full = w_gate.astype(jnp.float32)
    up_full = w_up.astype(jnp.float32)
    down_full = w_down.astype(jnp.float32)

    def group_step(totals, group_data):
        inputs_bf, grads_bf, weights_bf = group_data
        inputs = inputs_bf.astype(jnp.float32)
        slot_grads = grads_bf.astype(jnp.float32)
        weights = weights_bf.astype(jnp.float32)[:, :, None]
        pre_gate = jnp.einsum("prd,pdf->prf", inputs, gate_full)
        pre_up = jnp.einsum("prd,pdf->prf", inputs, up_full)
        silu_val, silu_slope = silu_parts(pre_gate)
        hidden = to_bf16_back(silu_val * pre_up)
        scaled = to_bf16_back(weights * slot_grads)
        backward = jnp.einsum("prd,pdf->prf", slot_grads, down_full)
        prob_part = to_bf16_back(jnp.sum((hidden * backward).reshape(N_EXPERT, per_expert, N_TENSOR, hidden_dev), axis=3))
        slot_prob = jnp.sum(prob_part, axis=2).astype(jnp.bfloat16)
        hidden_grad = weights * backward
        gate_grad = to_bf16_back(hidden_grad * pre_up * silu_slope)
        up_grad = to_bf16_back(hidden_grad * silu_val)
        down_part = to_bf16_back(jnp.einsum("prd,prf->pdf", scaled, hidden))
        gate_part = to_bf16_back(jnp.einsum("prd,prf->pdf", inputs, gate_grad))
        up_part = to_bf16_back(jnp.einsum("prd,prf->pdf", inputs, up_grad))
        gate_blocks = gate_grad.reshape(N_EXPERT, per_expert, N_TENSOR, hidden_dev)
        up_blocks = up_grad.reshape(N_EXPERT, per_expert, N_TENSOR, hidden_dev)
        input_part = jnp.einsum("prtf,pdtf->prtd", gate_blocks, gate_full.reshape(N_EXPERT, D, N_TENSOR, hidden_dev))
        input_part = input_part + jnp.einsum("prtf,pdtf->prtd", up_blocks, up_full.reshape(N_EXPERT, D, N_TENSOR, hidden_dev))
        slot_input = jnp.sum(to_bf16_back(input_part), axis=2).astype(jnp.bfloat16)
        new_totals = (totals[0] + gate_part, totals[1] + up_part, totals[2] + down_part)
        return new_totals, (slot_input, slot_prob)

    zeros_grad = jnp.zeros((N_EXPERT, D, FF), jnp.float32)
    group_inputs = (saved_inputs.reshape(N_DP, N_EXPERT, per_expert, D), slot_grad.reshape(N_DP, N_EXPERT, per_expert, D), slot_weight.reshape(N_DP, N_EXPERT, per_expert))
    totals, outputs = lax.scan(group_step, (zeros_grad, zeros_grad, zeros_grad), group_inputs)
    slot_input_all = jnp.concatenate([outputs[0].reshape(total_slots, D), jnp.zeros((1, D), jnp.bfloat16)], axis=0)
    slot_prob_all = jnp.concatenate([outputs[1].reshape(total_slots), jnp.zeros((1,), jnp.bfloat16)], axis=0)

    def add_position(summed, column):
        return summed + slot_input_all[column].astype(jnp.float32), None

    summed, unused = lax.scan(add_position, jnp.zeros((TOKENS, D), jnp.float32), slot_index.T)
    input_grad = summed.astype(jnp.bfloat16)
    prob_pos = slot_prob_all[slot_index].astype(jnp.float32)
    prob_grad = jnp.sum(onehot.astype(jnp.float32) * prob_pos[:, None, :], axis=2)
    return input_grad, prob_grad, totals[0], totals[1], totals[2]
```

```python
import jax
import jax.numpy as jnp
from jax import lax
from jax.experimental import pallas as pl
from jax.experimental.pallas import tpu as pltpu
from jax.sharding import PartitionSpec as P

EXP_DEV = 4
LANES = 256
CHUNK = 48
F32 = jnp.float32
BF16 = jnp.bfloat16
MESH = pl.DeviceIdType.MESH


def dot(left, right, dims=((1,), (0,))):
    return lax.dot_general(left, right, (dims, ((), ())), preferred_element_type=F32)


def iota(shape, dim):
    return lax.broadcasted_iota(jnp.int32, shape, dim)


def unpack_matrices(cap, pieces, n_exp):
    rows = n_exp * CHUNK
    at = iota((1, rows), 1)
    src = sum((at >= CHUNK * m).astype(jnp.int32) for m in range(1, n_exp))
    rest = at - CHUNK * src
    unpack = iota((rows, rows), 0) == rest * n_exp + src
    src = at % n_exp
    pack = iota((rows, rows), 0) == src * CHUNK + at // n_exp
    return unpack, pack


def kernel(
    sizes,
    grad_hbm, ids_hbm, probs_hbm, x_hbm, wg_hbm, wu_hbm, wd_hbm,
    out_ref, prob_out, gate_out, up_out, down_out,
    grad_v, ids_v, probs_v, xb, wg, wu, wd, ids_s, probs_s, prob_all, unpack, pack,
    send_buf, recv_buf, place, place_t,
    xt, slope_up, silu_s, hid_s, dy, scaled, gate_g, up_g, prob_s,
    xs_opp, xs_left, xs_right, xr1, xr2, ret_send, ret_recv, gather,
    dw, zbuf,
    load_sem, ysend, yrecv, xsend, xrecv, rsend, rrecv, wsend, wrecv, gsend, grecv, zsend, zrecv,
):
    n_dp, n_exp, n_ten, cap, top, d, hid = sizes
    share = grad_v.shape[0]
    pieces = d // LANES
    group = n_exp // 4
    slots = n_exp * cap
    half = slots // 2
    g, q, t = lax.axis_index("dp"), lax.axis_index("expert"), lax.axis_index("tensor")
    t_right, t_left, t_opp = (t + 1) % n_ten, (t + n_ten - 1) % n_ten, (t + 2) % n_ten
    g_right, g_left = (g + 1) % n_dp, (g + n_dp - 1) % n_dp

    def remote(src, dst, send, recv, axis, where):
        return pltpu.make_async_remote_copy(
            src_ref=src, dst_ref=dst, send_sem=send, recv_sem=recv,
            device_id={axis: where}, device_id_type=MESH,
        )

    tok = pl.ds(pl.multiple_of(t * share, share), share)
    loads = [
        pltpu.make_async_copy(ids_hbm, ids_v, load_sem.at[0]),
        pltpu.make_async_copy(probs_hbm, probs_v, load_sem.at[1]),
        pltpu.make_async_copy(grad_hbm.at[tok], grad_v, load_sem.at[2]),
        pltpu.make_async_copy(x_hbm, xb, load_sem.at[3]),
        pltpu.make_async_copy(wg_hbm, wg, load_sem.at[4]),
        pltpu.make_async_copy(wu_hbm, wu, load_sem.at[5]),
        pltpu.make_async_copy(wd_hbm, wd, load_sem.at[6]),
    ]
    for load in loads:
        load.start()
    barrier = pltpu.get_barrier_semaphore()

    def greet(k, carry):
        pl.semaphore_signal(barrier, inc=1, device_id={"expert": (q + k) % n_exp}, device_id_type=MESH)
        return carry

    lax.fori_loop(1, n_exp, greet, 0)
    for axis, where in (("tensor", t_right), ("tensor", t_left), ("dp", g_right), ("dp", g_left)):
        pl.semaphore_signal(barrier, inc=1, device_id={axis: where}, device_id_type=MESH)

    loads[0].wait()
    loads[1].wait()
    tokens_all = ids_s.shape[0]
    fill = jnp.zeros((128 - top, tokens_all), F32)
    ids_s[...] = jnp.concatenate([ids_v[...].astype(F32), fill], axis=0).T
    probs_s[...] = jnp.concatenate([probs_v[...], fill], axis=0).T
    ids = ids_s[tok, :]
    probs = probs_s[tok, :]
    lane = iota((share, 128), 1)
    name = (lane * EXP_DEV).astype(F32)
    routed = jnp.zeros((share, 128), F32)
    prob_tok = jnp.zeros((share, 128), F32)
    for k in range(top):
        hit = ids[:, k : k + 1] == name
        routed = routed + jnp.where(hit, 1.0, 0.0)
        prob_tok = prob_tok + jnp.where(hit, probs[:, k : k + 1], 0.0)
    lower = jnp.where(iota((share, share), 1) < iota((share, share), 0), 1.0, 0.0).astype(BF16)
    rank = dot(lower, routed.astype(BF16))
    code = jnp.where(routed > 0.0, rank, -128.0).astype(BF16)
    spread = ((iota((share, LANES), 1) % share) == iota((share, LANES), 0)).astype(BF16)
    code_x = dot(code, spread, ((0,), (0,)))
    rule = (iota((CHUNK, LANES), 0) - cap * (iota((CHUNK, LANES), 1) // share)).astype(F32)
    for p in range(n_exp):
        place[CHUNK * p : CHUNK * (p + 1), :] = jnp.where(code_x[p : p + 1, :] == rule, 1.0, 0.0).astype(BF16)
    loads[2].wait()
    grad = grad_v[...]
    stacked = jnp.concatenate(
        [grad[:, LANES * j : LANES * (j + 1)] for j in range(pieces)]
        + [jnp.concatenate([prob_tok, jnp.zeros((share, LANES - 128), F32)], axis=1).astype(BF16)],
        axis=0,
    )
    send_buf[...] = dot(place[...], stacked).astype(BF16).reshape(n_exp, CHUNK, LANES)
    pl.semaphore_wait(barrier, n_exp + 3)

    def partner(i):
        step = i // 2 + 1
        return (q + (i % 2) * (n_exp - 2 * step) + step) % n_exp

    def ycopy(i):
        p = partner(i)
        return remote(send_buf.at[p], recv_buf.at[0, q], ysend.at[p], yrecv.at[q], "expert", p)

    def ystart(i, carry):
        ycopy(i).start()
        return carry

    lax.fori_loop(0, n_exp - 1, ystart, 0)
    recv_buf[0, pl.ds(q, 1)] = send_buf[pl.ds(q, 1)]

    mine = q // group
    order = [mine, (mine + 1) % 4, (mine + 3) % 4, (mine + 2) % 4]

    def members(i):
        return pl.ds(order[i] * group, group)

    def ywait(i):
        def one(m, carry):
            src = order[i] * group + m

            @pl.when(src != q)
            def _():
                remote(send_buf.at[src], recv_buf.at[0, src], ysend.at[src], yrecv.at[src], "expert", src).wait_recv()

            return carry

        lax.fori_loop(0, group, one, 0)

    def xcopy(kind, i):
        m = members(i)
        if kind == 0:
            return remote(recv_buf.at[0, m], recv_buf.at[1, m], xsend.at[0, i], xrecv.at[0, i], "tensor", t_right)
        if kind == 1:
            return remote(recv_buf.at[0, m], recv_buf.at[2, m], xsend.at[1, i], xrecv.at[1, i], "tensor", t_left)
        if i < 2:
            return remote(recv_buf.at[1, m], recv_buf.at[3, m], xsend.at[2, i], xrecv.at[2, i], "tensor", t_right)
        return remote(recv_buf.at[2, m], recv_buf.at[3, m], xsend.at[2, i], xrecv.at[2, i], "tensor", t_left)

    def spread_group(i):
        ywait(i)
        xcopy(0, i).start()
        xcopy(1, i).start()

    def hand_on(i):
        xcopy(0 if i < 2 else 1, i).wait_recv()
        xcopy(2, i).start()

    def forward(first, last):
        rows = slice(first, last)
        x = xb[rows, :]
        pre_gate = dot(x, wg[...], nt)
        pre_up = dot(x, wu[...], nt)
        sig = jax.nn.sigmoid(pre_gate)
        silu = pre_gate * sig
        silu_s[rows, :] = silu
        slope_up[rows, :] = pre_up * (sig * (1.0 + pre_gate * (1.0 - sig)))
        hid_s[rows, :] = (silu * pre_up).astype(BF16)

    nt = ((1,), (1,))
    place_t[...] = place[...].T
    spread_group(0)
    opening, closing = unpack_matrices(cap, pieces + 1, n_exp)
    unpack[...] = opening.astype(BF16)
    pack[...] = closing.astype(BF16)
    spread_group(1)
    hand_on(0)
    for i in (3, 4, 5):
        loads[i].wait()
    forward(0, 2 * slots)
    spread_group(2)
    hand_on(1)
    forward(2 * slots, 4 * slots)
    spread_group(3)
    hand_on(2)
    xt[...] = xb[...].T
    hand_on(3)
    loads[6].wait()

    lane_q = iota((slots, LANES), 1) == q

    def rows_of(tt):
        return pl.ds(pl.multiple_of(tt * slots, 32), slots)

    def backward(rel, tt):
        rows = rows_of(tt)
        opened = dot(unpack[...], recv_buf[rel].reshape(n_exp * CHUNK, LANES))

        def piece(j):
            return opened[slots * j : slots * (j + 1), :]

        weight = jnp.sum(jnp.where(lane_q, piece(pieces), 0.0), axis=1, keepdims=True)
        for j in range(pieces):
            cols = slice(LANES * j, LANES * (j + 1))
            val = piece(j)
            dy[rows, cols] = val.astype(BF16)
            scaled[rows, cols] = (weight * val).astype(BF16)
        back = dot(dy[rows, :], wd[...], nt)
        prob = jnp.sum(hid_s[rows, :].astype(F32) * back, axis=1, keepdims=True)
        prob_s[rows, :] = jnp.broadcast_to(prob, (slots, 128))
        hidden_grad = weight * back
        gate_g[rows, :] = (hidden_grad * slope_up[rows, :]).astype(BF16)
        up_g[rows, :] = (hidden_grad * silu_s[rows, :]).astype(BF16)

    backward(0, t)
    for i in (2, 3):
        xcopy(0, i).wait_recv()
    backward(1, t_left)
    for i in (0, 1):
        xcopy(1, i).wait_recv()
    backward(2, t_right)
    for i in range(4):
        xcopy(2, i).wait_recv()
    backward(3, t_opp)

    def input_part(tt):
        rows = rows_of(tt)
        return dot(gate_g[rows, :], wg[...]) + dot(up_g[rows, :], wu[...])

    def put_part(ref, tt):
        ref[:, :d] = input_part(tt).astype(BF16)
        ref[:, d:] = prob_s[rows_of(tt), :].astype(BF16)

    lo, hi = pl.ds(0, half), pl.ds(half, half)
    first_right = remote(xs_opp.at[lo], xr1.at[0], rsend.at[0], rrecv.at[0], "tensor", t_right)
    first_left = remote(xs_opp.at[hi], xr1.at[1], rsend.at[1], rrecv.at[1], "tensor", t_left)
    plain_right = remote(xs_right.at[hi], xr2.at[0, hi], rsend.at[2], rrecv.at[2], "tensor", t_right)
    plain_left = remote(xs_left.at[lo], xr2.at[1, lo], rsend.at[3], rrecv.at[3], "tensor", t_left)
    added_right = remote(xs_right.at[lo], xr2.at[0, lo], rsend.at[4], rrecv.at[4], "tensor", t_right)
    added_left = remote(xs_left.at[hi], xr2.at[1, hi], rsend.at[5], rrecv.at[5], "tensor", t_left)

    put_part(xs_opp, t_opp)
    first_right.start()
    first_left.start()

    rows_z = d // n_dp
    last = n_dp - 2

    def zcopy(sub, s, src):
        return remote(
            src, zbuf.at[sub, s], zsend.at[sub, s], zrecv.at[sub, s], "dp", g_right if sub % 2 == 0 else g_left
        )

    def zrows(sub, s):
        owner = (g + 2 * n_dp - 1 - s) % n_dp if sub % 2 == 0 else (g + 1 + s) % n_dp
        return pl.ds(pl.multiple_of(owner * rows_z, 16), rows_z)

    def zfirst(sub):
        zcopy(sub, 0, dw.at[sub, zrows(sub, 0)]).start()

    def zstep(s, carry):
        for sub in range(4):
            zcopy(sub, s - 1, zbuf.at[sub, s - 1]).wait_recv()
            total = zbuf[sub, s - 1].astype(F32) + dw[sub, zrows(sub, s), :].astype(F32)
            zbuf[sub, s - 1] = total.astype(BF16)
            zcopy(sub, s, zbuf.at[sub, s - 1]).start()
        return carry

    def zsteps(first, end):
        lax.fori_loop(first, end, zstep, 0)

    dw[0] = dot(xt[...], gate_g[:, :LANES]).astype(BF16)
    zfirst(0)
    dw[1] = dot(xt[...], up_g[:, :LANES]).astype(BF16)
    zfirst(1)
    scaled_t = scaled[...].T
    dw[2] = dot(scaled_t, hid_s[:, :LANES]).astype(BF16)
    zfirst(2)
    rest = hid - LANES
    gate_up = jnp.concatenate([gate_g[:, LANES:], up_g[:, LANES:]], axis=1)
    dw[3, :, : 2 * rest] = dot(xt[...], gate_up).astype(BF16)
    dw[3, :, 2 * rest :] = jnp.concatenate(
        [dot(scaled_t, hid_s[:, LANES:]), jnp.zeros((d, LANES - 3 * rest), F32)], axis=1
    ).astype(BF16)
    zfirst(3)
    put_part(xs_right, t_right)
    plain_right.start()
    put_part(xs_left, t_left)
    plain_left.start()

    zsteps(1, 3)
    first_right.wait_recv()
    xs_right[lo, :] = (xs_right[lo, :].astype(F32) + xr1[0].astype(F32)).astype(BF16)
    added_right.start()
    first_left.wait_recv()
    xs_left[hi, :] = (xs_left[hi, :].astype(F32) + xr1[1].astype(F32)).astype(BF16)
    added_left.start()

    zsteps(3, 6)
    for copy in (plain_right, plain_left, added_right, added_left):
        copy.wait_recv()
    slot_input = input_part(t) + xr2[0, :, :d].astype(F32) + xr2[1, :, :d].astype(F32)
    slot_prob = prob_s[rows_of(t), :] + xr2[0, :, d:].astype(F32) + xr2[1, :, d:].astype(F32)
    slot_prob = jnp.where(lane_q, jnp.concatenate([slot_prob] * (LANES // 128), axis=1), 0.0)
    pile = jnp.concatenate(
        [slot_input[:, LANES * j : LANES * (j + 1)] for j in range(pieces)] + [slot_prob], axis=0
    ).astype(BF16)
    ret_send[...] = dot(pack[...], pile).astype(BF16).reshape(n_exp, CHUNK, LANES)

    def wcopy(i):
        p = partner(i)
        return remote(ret_send.at[p], ret_recv.at[q], wsend.at[p], wrecv.at[q], "expert", p)

    def wstart(i, carry):
        wcopy(i).start()
        return carry

    lax.fori_loop(0, n_exp - 1, wstart, 0)
    ret_recv[pl.ds(q, 1)] = ret_send[pl.ds(q, 1)]

    zsteps(6, 10)

    def wwait(i, carry):
        p = partner(i)
        remote(ret_send.at[p], ret_recv.at[p], wsend.at[p], wrecv.at[p], "expert", p).wait_recv()
        return carry

    lax.fori_loop(0, n_exp - 1, wwait, 0)
    tokens = dot(place_t[...], ret_recv[...].reshape(n_exp * CHUNK, LANES))
    for j in range(pieces):
        gather[0, :, LANES * j : LANES * (j + 1)] = tokens[share * j : share * (j + 1), :].astype(BF16)
    prob_pos = tokens[share * pieces :, :128]
    prob_tk = jnp.zeros((share, 128), F32)
    for k in range(top):
        val = jnp.sum(jnp.where(ids[:, k : k + 1] == name, prob_pos, 0.0), axis=1, keepdims=True)
        prob_tk = jnp.where(lane == k, val, prob_tk)
    gather[0, :, d:] = prob_tk.astype(BF16)

    low, high = pl.ds(0, share // 2), pl.ds(share // 2, share // 2)
    to_right = remote(gather.at[0], gather.at[1], gsend.at[0], grecv.at[0], "tensor", t_right)
    to_left = remote(gather.at[0], gather.at[2], gsend.at[1], grecv.at[1], "tensor", t_left)
    on_right = remote(gather.at[1, low], gather.at[3, low], gsend.at[2], grecv.at[2], "tensor", t_right)
    on_left = remote(gather.at[2, high], gather.at[3, high], gsend.at[3], grecv.at[3], "tensor", t_left)
    to_right.start()
    to_left.start()

    def put_tokens(rel, tt):
        rows = pl.ds(pl.multiple_of(tt * share, share), share)
        out_ref[rows, :] = gather[rel, :, :d]
        prob_all[rows, :] = gather[rel, :, d:].astype(F32)

    zsteps(10, 12)
    put_tokens(0, t)
    to_right.wait_recv()
    on_right.start()
    to_left.wait_recv()
    on_left.start()
    zsteps(12, last + 1)
    put_tokens(1, t_left)
    put_tokens(2, t_right)
    on_right.wait_recv()
    on_left.wait_recv()
    put_tokens(3, t_opp)

    own = []
    for sub in range(4):
        zcopy(sub, last, zbuf.at[sub, last]).wait_recv()
        own.append(zbuf[sub, last].astype(F32) + dw[sub, zrows(sub, last + 1), :].astype(F32))
    own = [jnp.concatenate([o, jnp.zeros((128 - rows_z, LANES), F32)], axis=0).T[:, :rows_z] for o in own]
    gate_out[:LANES, :] = own[0]
    gate_out[LANES:, :] = own[3][:rest]
    up_out[:LANES, :] = own[1]
    up_out[LANES:, :] = own[3][rest : 2 * rest]
    down_out[:LANES, :] = own[2]
    down_out[LANES:, :] = own[3][2 * rest : 3 * rest]
    prob_out[...] = prob_all[...].T[:top]

    def sent(i, carry):
        ycopy(i).wait_send()
        wcopy(i).wait_send()
        return carry

    lax.fori_loop(0, n_exp - 1, sent, 0)
    for kind in range(3):
        for i in range(4):
            xcopy(kind, i).wait_send()
    for copy in (first_right, first_left, plain_right, plain_left, added_right, added_left):
        copy.wait_send()
    for copy in (to_right, to_left, on_right, on_left):
        copy.wait_send()

    def zsent(s, carry):
        for sub in range(4):
            zcopy(sub, s, zbuf.at[sub, s]).wait_send()
        return carry

    lax.fori_loop(0, n_dp - 1, zsent, 0)


def shards(grad_out, expert_ids, gate_probs, saved_inputs, w_gate, w_up, w_down):
    n_dp, n_exp, n_ten = lax.axis_size("dp"), lax.axis_size("expert"), lax.axis_size("tensor")
    tok_rows, d = grad_out.shape
    cap, top, hid = saved_inputs.shape[4], expert_ids.shape[1], w_gate.shape[2]
    share = tok_rows // n_ten
    slots = n_exp * cap
    total = n_ten * slots
    wide = d + 128
    rows_z = d // n_dp
    vmem = pltpu.VMEM
    dma = pltpu.SemaphoreType.DMA
    outs = pl.pallas_call(
        lambda *refs: kernel((n_dp, n_exp, n_ten, cap, top, d, hid), *refs),
        out_shape=(
            jax.ShapeDtypeStruct((tok_rows, d), BF16),
            jax.ShapeDtypeStruct((top, tok_rows), F32),
            jax.ShapeDtypeStruct((hid, rows_z), F32),
            jax.ShapeDtypeStruct((hid, rows_z), F32),
            jax.ShapeDtypeStruct((hid, rows_z), F32),
        ),
        in_specs=[pl.BlockSpec(memory_space=pl.ANY)] * 7,
        out_specs=(pl.BlockSpec(memory_space=pltpu.VMEM),) * 5,
        scratch_shapes=[
            vmem((share, d), BF16),
            vmem((top, tok_rows), jnp.int32),
            vmem((top, tok_rows), F32),
            vmem((total, d), BF16),
            vmem((hid, d), BF16),
            vmem((hid, d), BF16),
            vmem((hid, d), BF16),
            vmem((tok_rows, 128), F32),
            vmem((tok_rows, 128), F32),
            vmem((tok_rows, 128), F32),
            vmem((n_exp * CHUNK, n_exp * CHUNK), BF16),
            vmem((n_exp * CHUNK, n_exp * CHUNK), BF16),
            vmem((n_exp, CHUNK, LANES), BF16),
            vmem((4, n_exp, CHUNK, LANES), BF16),
            vmem((n_exp * CHUNK, LANES), BF16),
            vmem((LANES, n_exp * CHUNK), BF16),
            vmem((d, total), BF16),
            vmem((total, hid), F32),
            vmem((total, hid), F32),
            vmem((total, hid), BF16),
            vmem((total, d), BF16),
            vmem((total, d), BF16),
            vmem((total, hid), BF16),
            vmem((total, hid), BF16),
            vmem((total, 128), F32),
            vmem((slots, wide), BF16),
            vmem((slots, wide), BF16),
            vmem((slots, wide), BF16),
            vmem((2, slots // 2, wide), BF16),
            vmem((2, slots, wide), BF16),
            vmem((n_exp, CHUNK, LANES), BF16),
            vmem((n_exp, CHUNK, LANES), BF16),
            vmem((4, share, wide), BF16),
            vmem((4, d, LANES), BF16),
            vmem((4, n_dp - 1, rows_z, LANES), BF16),
            dma((7,)),
            dma((n_exp,)),
            dma((n_exp,)),
            dma((3, 4)),
            dma((3, 4)),
            dma((6,)),
            dma((6,)),
            dma((n_exp,)),
            dma((n_exp,)),
            dma((4,)),
            dma((4,)),
            dma((4, n_dp - 1)),
            dma((4, n_dp - 1)),
        ],
        compiler_params=pltpu.CompilerParams(
            collective_id=0, has_side_effects=True, vmem_limit_bytes=56 * 1024 * 1024
        ),
        name="expert_backward",
    )(
        grad_out,
        expert_ids.T,
        gate_probs.T,
        saved_inputs.transpose(0, 1, 2, 4, 3, 5).reshape(total, d),
        w_gate[0].T,
        w_up[0].T,
        w_down[0].T,
    )
    return outs[0], outs[1].T, outs[2].T[None], outs[3].T[None], outs[4].T[None]


def solution(mesh):
    return jax.shard_map(
        shards,
        mesh=mesh,
        in_specs=(
            P(("dp", "expert"), None),
            P(("dp", "expert"), None),
            P(("dp", "expert"), None),
            P("dp", "expert", None, None, None, None),
            P("expert", None, "tensor"),
            P("expert", None, "tensor"),
            P("expert", None, "tensor"),
        ),
        out_specs=(
            P(("dp", "expert"), None),
            P(("dp", "expert"), None),
            P("expert", "dp", "tensor"),
            P("expert", "dp", "tensor"),
            P("expert", "dp", "tensor"),
        ),
        check_vma=False,
    )
```

```python
import jax
import jax.numpy as jnp
from jax import lax
from jax.experimental import pallas as pl
from jax.experimental.pallas import tpu as pltpu
from jax.sharding import PartitionSpec as P

EXP_DEV = 4
LANES = 256
CHUNK = 48
F32 = jnp.float32
BF16 = jnp.bfloat16
MESH = pl.DeviceIdType.MESH


def dot(left, right, dims=((1,), (0,))):
    return lax.dot_general(left, right, (dims, ((), ())), preferred_element_type=F32)


def iota(shape, dim):
    return lax.broadcasted_iota(jnp.int32, shape, dim)


def unpack_matrices(cap, pieces, n_exp):
    rows = n_exp * CHUNK
    at = iota((1, rows), 1)
    src = sum((at >= CHUNK * m).astype(jnp.int32) for m in range(1, n_exp))
    rest = at - CHUNK * src
    unpack = iota((rows, rows), 0) == rest * n_exp + src
    src = at % n_exp
    pack = iota((rows, rows), 0) == src * CHUNK + at // n_exp
    return unpack, pack


def kernel(
    sizes,
    grad_hbm, ids_hbm, probs_hbm, x_hbm, wg_hbm, wu_hbm, wd_hbm,
    out_ref, prob_out, gate_out, up_out, down_out,
    grad_v, ids_v, probs_v, xb, wg, wu, wd, ids_s, probs_s, prob_all, unpack, pack,
    send_buf, recv_buf, place, place_t,
    xt, st, slope_up, silu_s, hid_s, hid_r, gate_g, up_g, gate_up, hid_rest, prob_s, own_part,
    xs_opp, xs_left, xs_right, xr1, xr2, ret_send, ret_recv, gather,
    zfirst, zbuf,
    load_sem, ysend, yrecv, xsend, xrecv, rsend, rrecv, wsend, wrecv, gsend, grecv, zsend, zrecv,
):
    n_dp, n_exp, n_ten, cap, top, d, hid = sizes
    share = grad_v.shape[0]
    pieces = d // LANES
    group = 2
    groups = n_exp // group
    rest = hid - LANES
    slots = n_exp * cap
    half = slots // 2
    g, q, t = lax.axis_index("dp"), lax.axis_index("expert"), lax.axis_index("tensor")
    t_right, t_left, t_opp = (t + 1) % n_ten, (t + n_ten - 1) % n_ten, (t + 2) % n_ten
    g_right, g_left = (g + 1) % n_dp, (g + n_dp - 1) % n_dp

    def remote(src, dst, send, recv, axis, where):
        return pltpu.make_async_remote_copy(
            src_ref=src, dst_ref=dst, send_sem=send, recv_sem=recv,
            device_id={axis: where}, device_id_type=MESH,
        )

    tok = pl.ds(pl.multiple_of(t * share, share), share)
    loads = [
        pltpu.make_async_copy(ids_hbm, ids_v, load_sem.at[0]),
        pltpu.make_async_copy(probs_hbm, probs_v, load_sem.at[1]),
        pltpu.make_async_copy(grad_hbm.at[tok], grad_v, load_sem.at[2]),
        pltpu.make_async_copy(x_hbm, xb, load_sem.at[3]),
        pltpu.make_async_copy(wg_hbm, wg, load_sem.at[4]),
        pltpu.make_async_copy(wu_hbm, wu, load_sem.at[5]),
        pltpu.make_async_copy(wd_hbm, wd, load_sem.at[6]),
    ]
    for load in loads:
        load.start()
    barrier = pltpu.get_barrier_semaphore()

    def greet(k, carry):
        pl.semaphore_signal(barrier, inc=1, device_id={"expert": (q + k) % n_exp}, device_id_type=MESH)
        return carry

    lax.fori_loop(1, n_exp, greet, 0)
    for axis, where in (("tensor", t_right), ("tensor", t_left), ("dp", g_right), ("dp", g_left)):
        pl.semaphore_signal(barrier, inc=1, device_id={axis: where}, device_id_type=MESH)

    loads[0].wait()
    loads[1].wait()
    tokens_all = ids_s.shape[0]
    fill = jnp.zeros((128 - top, tokens_all), F32)
    ids_s[...] = jnp.concatenate([ids_v[...].astype(F32), fill], axis=0).T
    probs_s[...] = jnp.concatenate([probs_v[...], fill], axis=0).T
    ids = ids_s[tok, :]
    probs = probs_s[tok, :]
    lane = iota((share, 128), 1)
    name = (lane * EXP_DEV).astype(F32)
    routed = jnp.zeros((share, 128), F32)
    prob_tok = jnp.zeros((share, 128), F32)
    for k in range(top):
        hit = ids[:, k : k + 1] == name
        routed = routed + jnp.where(hit, 1.0, 0.0)
        prob_tok = prob_tok + jnp.where(hit, probs[:, k : k + 1], 0.0)
    lower = jnp.where(iota((share, share), 1) < iota((share, share), 0), 1.0, 0.0).astype(BF16)
    rank = dot(lower, routed.astype(BF16))
    code = jnp.where(routed > 0.0, rank, -128.0).astype(BF16)
    spread = ((iota((share, LANES), 1) % share) == iota((share, LANES), 0)).astype(BF16)
    code_x = dot(code, spread, ((0,), (0,)))
    rule = (iota((CHUNK, LANES), 0) - cap * (iota((CHUNK, LANES), 1) // share)).astype(F32)
    for p in range(n_exp):
        place[CHUNK * p : CHUNK * (p + 1), :] = jnp.where(code_x[p : p + 1, :] == rule, 1.0, 0.0).astype(BF16)
    loads[2].wait()
    grad = grad_v[...]
    stacked = jnp.concatenate(
        [grad[:, LANES * j : LANES * (j + 1)] for j in range(pieces)]
        + [jnp.concatenate([prob_tok, jnp.zeros((share, LANES - 128), F32)], axis=1).astype(BF16)],
        axis=0,
    )
    send_buf[...] = dot(place[...], stacked).astype(BF16).reshape(n_exp, CHUNK, LANES)
    pl.semaphore_wait(barrier, n_exp + 3)

    def partner(i):
        step = i // 2 + 1
        return (q + (i % 2) * (n_exp - 2 * step) + step) % n_exp

    def ycopy(i):
        p = partner(i)
        return remote(send_buf.at[p], recv_buf.at[0, q], ysend.at[p], yrecv.at[q], "expert", p)

    def ystart(i, carry):
        ycopy(i).start()
        return carry

    lax.fori_loop(0, n_exp - 1, ystart, 0)
    recv_buf[0, pl.ds(q, 1)] = send_buf[pl.ds(q, 1)]

    mine = q // group
    order = [mine]
    for away in range(1, groups // 2):
        order += [(mine + away) % groups, (mine + groups - away) % groups]
    order.append((mine + groups // 2) % groups)

    def members(i):
        return pl.ds(order[i] * group, group)

    def ywait(i):
        def one(m, carry):
            src = order[i] * group + m

            @pl.when(src != q)
            def _():
                remote(send_buf.at[src], recv_buf.at[0, src], ysend.at[src], yrecv.at[src], "expert", src).wait_recv()

            return carry

        lax.fori_loop(0, group, one, 0)

    def xcopy(kind, i):
        m = members(i)
        if kind == 0:
            return remote(recv_buf.at[0, m], recv_buf.at[1, m], xsend.at[0, i], xrecv.at[0, i], "tensor", t_right)
        if kind == 1:
            return remote(recv_buf.at[0, m], recv_buf.at[2, m], xsend.at[1, i], xrecv.at[1, i], "tensor", t_left)
        if i % 2 == 0:
            return remote(recv_buf.at[1, m], recv_buf.at[3, m], xsend.at[2, i], xrecv.at[2, i], "tensor", t_right)
        return remote(recv_buf.at[2, m], recv_buf.at[3, m], xsend.at[2, i], xrecv.at[2, i], "tensor", t_left)

    def spread_group(i):
        ywait(i)
        xcopy(0, i).start()
        xcopy(1, i).start()

    def hand_on(i):
        xcopy(i % 2, i).wait_recv()
        xcopy(2, i).start()

    def forward(first, last):
        rows = slice(first, last)
        x = xb[rows, :]
        pre_gate = dot(x, wg[...], nt)
        pre_up = dot(x, wu[...], nt)
        sig = jax.nn.sigmoid(pre_gate)
        silu = pre_gate * sig
        silu_s[rows, :] = silu
        slope_up[rows, :] = pre_up * (sig * (1.0 + pre_gate * (1.0 - sig)))
        hid_s[rows, :] = (silu * pre_up).astype(BF16)

    nt = ((1,), (1,))
    spread_group(0)
    place_t[...] = place[...].T
    spread_group(1)
    opening, closing = unpack_matrices(cap, pieces + 1, n_exp)
    unpack[...] = opening.astype(BF16)
    hand_on(0)
    spread_group(2)
    pack[...] = closing.astype(BF16)
    hand_on(1)
    for i in (3, 4, 5):
        loads[i].wait()
    spread_group(3)
    hand_on(2)
    forward(0, 2 * slots)
    spread_group(4)
    hand_on(3)
    forward(2 * slots, 4 * slots)
    spread_group(5)
    hand_on(4)
    xt[...] = xb[...].T
    loads[6].wait()
    spread_group(6)
    hand_on(5)
    spread_group(7)
    hand_on(6)

    lane_q = iota((slots, LANES), 1) == q
    blank = 128 - slots

    def rows_of(tt):
        return pl.ds(pl.multiple_of(tt * slots, 32), slots)

    def backward(rel, tt):
        rows = rows_of(tt)
        opened = dot(unpack[...], recv_buf[rel].reshape(n_exp * CHUNK, LANES))

        def piece(j):
            return opened[slots * j : slots * (j + 1), :]

        weight = jnp.sum(jnp.where(lane_q, piece(pieces), 0.0), axis=1, keepdims=True)
        dy = jnp.concatenate([piece(j) for j in range(pieces)], axis=1)
        at = slice(128 * rel, 128 * (rel + 1))
        st[:, at] = jnp.concatenate([(weight * dy).astype(BF16), jnp.zeros((blank, d), BF16)], axis=0).T
        hid_r[at, :] = jnp.concatenate([hid_s[rows, :], jnp.zeros((blank, hid), BF16)], axis=0)
        back = dot(dy.astype(BF16), wd[...], nt)
        prob = jnp.sum(hid_s[rows, :].astype(F32) * back, axis=1, keepdims=True)
        prob_s[rows, :] = jnp.broadcast_to(prob, (slots, 128))
        hidden_grad = weight * back
        gate_g[rows, :] = (hidden_grad * slope_up[rows, :]).astype(BF16)
        up_g[rows, :] = (hidden_grad * silu_s[rows, :]).astype(BF16)

    backward(0, t)
    hand_on(7)
    for i in range(1, groups, 2):
        xcopy(0, i).wait_recv()
    backward(1, t_left)
    for i in range(0, groups, 2):
        xcopy(1, i).wait_recv()
    backward(2, t_right)
    for i in range(groups):
        xcopy(2, i).wait_recv()
    backward(3, t_opp)
    gate_up[...] = jnp.concatenate([gate_g[:, LANES:], up_g[:, LANES:]], axis=1)
    hid_rest[...] = jnp.concatenate([hid_r[:, LANES:], jnp.zeros((4 * 128, 128 - rest), BF16)], axis=1)

    def input_part(tt):
        rows = rows_of(tt)
        return dot(gate_g[rows, :], wg[...]) + dot(up_g[rows, :], wu[...])

    def put_part(ref, tt):
        ref[:, :d] = input_part(tt).astype(BF16)
        ref[:, d:] = prob_s[rows_of(tt), :].astype(BF16)

    lo, hi = pl.ds(0, half), pl.ds(half, half)
    first_right = remote(xs_opp.at[lo], xr1.at[0], rsend.at[0], rrecv.at[0], "tensor", t_right)
    first_left = remote(xs_opp.at[hi], xr1.at[1], rsend.at[1], rrecv.at[1], "tensor", t_left)
    plain_right = remote(xs_right.at[hi], xr2.at[0, hi], rsend.at[2], rrecv.at[2], "tensor", t_right)
    plain_left = remote(xs_left.at[lo], xr2.at[1, lo], rsend.at[3], rrecv.at[3], "tensor", t_left)
    added_right = remote(xs_right.at[lo], xr2.at[0, lo], rsend.at[4], rrecv.at[4], "tensor", t_right)
    added_left = remote(xs_left.at[hi], xr2.at[1, hi], rsend.at[5], rrecv.at[5], "tensor", t_left)

    rows_z = d // n_dp
    hops = n_dp // 2

    def zcopy(way, sub, s, src):
        return remote(
            src, zbuf.at[way, sub, s], zsend.at[way, sub, s], zrecv.at[way, sub, s], "dp", g_left if way else g_right
        )

    def zrows(way, s):
        owner = (g + hops + s) % n_dp if way else (g + n_dp + hops - s) % n_dp
        return pl.ds(pl.multiple_of(owner * rows_z, 16), rows_z)

    def term(sub, chunks):
        def left(ref):
            return jnp.concatenate([ref[rows, :] for rows in chunks], axis=0)

        if sub == 0:
            return dot(left(xt), gate_g[:, :LANES])
        if sub == 1:
            return dot(left(xt), up_g[:, :LANES])
        if sub == 2:
            return dot(left(st), hid_r[:, :LANES])
        return jnp.concatenate([dot(left(xt), gate_up[...]), dot(left(st), hid_rest[...])], axis=1)

    def zpiece(s, sub, got):
        terms = term(sub, [zrows(0, s), zrows(1, s)])
        for way in range(2):
            total = terms[rows_z * way : rows_z * (way + 1), :]
            slot = zbuf.at[way, sub, s - 1]
            if got[way]:
                zcopy(way, sub, s - 1, slot).wait_recv()
                total = total + slot[...].astype(F32)
            slot[...] = total.astype(BF16)
            zcopy(way, sub, s, slot).start()

    def zsteps(first, end):
        def step(s, carry):
            for sub in range(4):
                zpiece(s, sub, (True, True))
            return carry

        lax.fori_loop(first, end, step, 0)

    for sub in (0, 2, 1, 3):
        zfirst[sub] = term(sub, [zrows(0, 0)]).astype(BF16)
        zcopy(sub // 2, sub, 0, zfirst.at[sub]).start()
    put_part(xs_opp, t_opp)
    first_right.start()
    first_left.start()

    for sub in range(4):
        zpiece(1, sub, (sub < 2, sub >= 2))
    put_part(xs_right, t_right)
    plain_right.start()
    put_part(xs_left, t_left)
    plain_left.start()
    zsteps(2, 3)
    first_right.wait_recv()
    xs_right[lo, :] = (xs_right[lo, :].astype(F32) + xr1[0].astype(F32)).astype(BF16)
    added_right.start()
    first_left.wait_recv()
    xs_left[hi, :] = (xs_left[hi, :].astype(F32) + xr1[1].astype(F32)).astype(BF16)
    added_left.start()
    own_part[...] = input_part(t)

    zsteps(3, 4)
    for copy in (plain_right, plain_left, added_right, added_left):
        copy.wait_recv()
    slot_input = own_part[...] + xr2[0, :, :d].astype(F32) + xr2[1, :, :d].astype(F32)
    slot_prob = prob_s[rows_of(t), :] + xr2[0, :, d:].astype(F32) + xr2[1, :, d:].astype(F32)
    slot_prob = jnp.where(lane_q, jnp.concatenate([slot_prob] * (LANES // 128), axis=1), 0.0)
    pile = jnp.concatenate(
        [slot_input[:, LANES * j : LANES * (j + 1)] for j in range(pieces)] + [slot_prob], axis=0
    ).astype(BF16)
    ret_send[...] = dot(pack[...], pile).astype(BF16).reshape(n_exp, CHUNK, LANES)

    def wcopy(i):
        p = partner(i)
        return remote(ret_send.at[p], ret_recv.at[q], wsend.at[p], wrecv.at[q], "expert", p)

    def wstart(i, carry):
        wcopy(i).start()
        return carry

    lax.fori_loop(0, n_exp - 1, wstart, 0)
    ret_recv[pl.ds(q, 1)] = ret_send[pl.ds(q, 1)]

    zsteps(4, 6)

    def wwait(i, carry):
        p = partner(i)
        remote(ret_send.at[p], ret_recv.at[p], wsend.at[p], wrecv.at[p], "expert", p).wait_recv()
        return carry

    lax.fori_loop(0, n_exp - 1, wwait, 0)
    tokens = dot(place_t[...], ret_recv[...].reshape(n_exp * CHUNK, LANES))
    for j in range(pieces):
        gather[0, :, LANES * j : LANES * (j + 1)] = tokens[share * j : share * (j + 1), :].astype(BF16)
    prob_pos = tokens[share * pieces :, :128]
    prob_tk = jnp.zeros((share, 128), F32)
    for k in range(top):
        val = jnp.sum(jnp.where(ids[:, k : k + 1] == name, prob_pos, 0.0), axis=1, keepdims=True)
        prob_tk = jnp.where(lane == k, val, prob_tk)
    gather[0, :, d:] = prob_tk.astype(BF16)

    low, high = pl.ds(0, share // 2), pl.ds(share // 2, share // 2)
    to_right = remote(gather.at[0], gather.at[1], gsend.at[0], grecv.at[0], "tensor", t_right)
    to_left = remote(gather.at[0], gather.at[2], gsend.at[1], grecv.at[1], "tensor", t_left)
    on_right = remote(gather.at[1, low], gather.at[3, low], gsend.at[2], grecv.at[2], "tensor", t_right)
    on_left = remote(gather.at[2, high], gather.at[3, high], gsend.at[3], grecv.at[3], "tensor", t_left)
    to_right.start()
    to_left.start()

    def put_tokens(rel, tt):
        rows = pl.ds(pl.multiple_of(tt * share, share), share)
        out_ref[rows, :] = gather[rel, :, :d]
        prob_all[rows, :] = gather[rel, :, d:].astype(F32)

    put_tokens(0, t)
    zsteps(6, 7)
    to_right.wait_recv()
    on_right.start()
    to_left.wait_recv()
    on_left.start()
    zsteps(7, hops)
    put_tokens(1, t_left)
    put_tokens(2, t_right)
    on_right.wait_recv()
    on_left.wait_recv()
    put_tokens(3, t_opp)

    own = []
    for sub in range(4):
        total = term(sub, [zrows(0, hops)])
        for way in range(2):
            zcopy(way, sub, hops - 1, zbuf.at[way, sub, hops - 1]).wait_recv()
            total = total + zbuf[way, sub, hops - 1].astype(F32)
        own.append(total)
    own = [jnp.concatenate([o, jnp.zeros((128 - rows_z, LANES), F32)], axis=0).T[:, :rows_z] for o in own]
    gate_out[:LANES, :] = own[0]
    gate_out[LANES:, :] = own[3][:rest]
    up_out[:LANES, :] = own[1]
    up_out[LANES:, :] = own[3][rest : 2 * rest]
    down_out[:LANES, :] = own[2]
    down_out[LANES:, :] = own[3][2 * rest : 3 * rest]
    prob_out[...] = prob_all[...].T[:top]

    def sent(i, carry):
        ycopy(i).wait_send()
        wcopy(i).wait_send()
        return carry

    lax.fori_loop(0, n_exp - 1, sent, 0)
    for kind in range(3):
        for i in range(groups):
            xcopy(kind, i).wait_send()
    for copy in (first_right, first_left, plain_right, plain_left, added_right, added_left):
        copy.wait_send()
    for copy in (to_right, to_left, on_right, on_left):
        copy.wait_send()

    for sub in range(4):
        zcopy(sub // 2, sub, 0, zfirst.at[sub]).wait_send()

    def zsent(s, carry):
        for way in range(2):
            for sub in range(4):
                zcopy(way, sub, s, zbuf.at[way, sub, s]).wait_send()
        return carry

    lax.fori_loop(1, hops, zsent, 0)


def finish(*refs):
    for src, dst in zip(refs[:5], refs[5:]):
        dst[...] = src[...]


def shards(grad_out, expert_ids, gate_probs, saved_inputs, w_gate, w_up, w_down):
    n_dp, n_exp, n_ten = lax.axis_size("dp"), lax.axis_size("expert"), lax.axis_size("tensor")
    tok_rows, d = grad_out.shape
    cap, top, hid = saved_inputs.shape[4], expert_ids.shape[1], w_gate.shape[2]
    share = tok_rows // n_ten
    slots = n_exp * cap
    total = n_ten * slots
    wide = d + 128
    rows_z = d // n_dp
    vmem = pltpu.VMEM
    dma = pltpu.SemaphoreType.DMA
    shapes = (
        jax.ShapeDtypeStruct((tok_rows, d), BF16),
        jax.ShapeDtypeStruct((top, tok_rows), F32),
        jax.ShapeDtypeStruct((hid, rows_z), F32),
        jax.ShapeDtypeStruct((hid, rows_z), F32),
        jax.ShapeDtypeStruct((hid, rows_z), F32),
    )
    outs = pl.pallas_call(
        lambda *refs: kernel((n_dp, n_exp, n_ten, cap, top, d, hid), *refs),
        out_shape=shapes,
        in_specs=[pl.BlockSpec(memory_space=pl.ANY)] * 7,
        out_specs=(pl.BlockSpec(memory_space=pltpu.VMEM),) * 5,
        scratch_shapes=[
            vmem((share, d), BF16),
            vmem((top, tok_rows), jnp.int32),
            vmem((top, tok_rows), F32),
            vmem((total, d), BF16),
            vmem((hid, d), BF16),
            vmem((hid, d), BF16),
            vmem((hid, d), BF16),
            vmem((tok_rows, 128), F32),
            vmem((tok_rows, 128), F32),
            vmem((tok_rows, 128), F32),
            vmem((n_exp * CHUNK, n_exp * CHUNK), BF16),
            vmem((n_exp * CHUNK, n_exp * CHUNK), BF16),
            vmem((n_exp, CHUNK, LANES), BF16),
            vmem((4, n_exp, CHUNK, LANES), BF16),
            vmem((n_exp * CHUNK, LANES), BF16),
            vmem((LANES, n_exp * CHUNK), BF16),
            vmem((d, total), BF16),
            vmem((d, 4 * 128), BF16),
            vmem((total, hid), F32),
            vmem((total, hid), F32),
            vmem((total, hid), BF16),
            vmem((4 * 128, hid), BF16),
            vmem((total, hid), BF16),
            vmem((total, hid), BF16),
            vmem((total, 128), BF16),
            vmem((4 * 128, 128), BF16),
            vmem((total, 128), F32),
            vmem((slots, d), F32),
            vmem((slots, wide), BF16),
            vmem((slots, wide), BF16),
            vmem((slots, wide), BF16),
            vmem((2, slots // 2, wide), BF16),
            vmem((2, slots, wide), BF16),
            vmem((n_exp, CHUNK, LANES), BF16),
            vmem((n_exp, CHUNK, LANES), BF16),
            vmem((4, share, wide), BF16),
            vmem((4, rows_z, LANES), BF16),
            vmem((2, 4, n_dp // 2, rows_z, LANES), BF16),
            dma((7,)),
            dma((n_exp,)),
            dma((n_exp,)),
            dma((3, n_exp // 2)),
            dma((3, n_exp // 2)),
            dma((6,)),
            dma((6,)),
            dma((n_exp,)),
            dma((n_exp,)),
            dma((4,)),
            dma((4,)),
            dma((2, 4, n_dp // 2)),
            dma((2, 4, n_dp // 2)),
        ],
        compiler_params=pltpu.CompilerParams(
            collective_id=0, has_side_effects=True, vmem_limit_bytes=56 * 1024 * 1024
        ),
        name="expert_backward",
    )(
        grad_out,
        expert_ids.T,
        gate_probs.T,
        saved_inputs.transpose(0, 1, 2, 4, 3, 5).reshape(total, d),
        w_gate[0].T,
        w_up[0].T,
        w_down[0].T,
    )
    outs = pl.pallas_call(
        finish,
        out_shape=shapes,
        in_specs=[pl.BlockSpec(memory_space=pltpu.VMEM)] * 5,
        out_specs=(pl.BlockSpec(memory_space=pltpu.VMEM),) * 5,
        name="write_results",
    )(*outs)
    return outs[0], outs[1].T, outs[2].T[None], outs[3].T[None], outs[4].T[None]


def solution(mesh):
    return jax.shard_map(
        shards,
        mesh=mesh,
        in_specs=(
            P(("dp", "expert"), None),
            P(("dp", "expert"), None),
            P(("dp", "expert"), None),
            P("dp", "expert", None, None, None, None),
            P("expert", None, "tensor"),
            P("expert", None, "tensor"),
            P("expert", None, "tensor"),
        ),
        out_specs=(
            P(("dp", "expert"), None),
            P(("dp", "expert"), None),
            P("expert", "dp", "tensor"),
            P("expert", "dp", "tensor"),
            P("expert", "dp", "tensor"),
        ),
        check_vma=False,
    )
```

```python
import jax
import jax.numpy as jnp
from jax import lax
from jax.experimental import pallas as pl
from jax.experimental.pallas import tpu as pltpu
from jax.sharding import PartitionSpec as P

EXP_DEV = 4
LANES = 256
CHUNK = 48
F32 = jnp.float32
BF16 = jnp.bfloat16
MESH = pl.DeviceIdType.MESH


def dot(left, right, dims=((1,), (0,))):
    return lax.dot_general(left, right, (dims, ((), ())), preferred_element_type=F32)


def iota(shape, dim):
    return lax.broadcasted_iota(jnp.int32, shape, dim)


def unpack_matrices(cap, pieces, n_exp):
    rows = n_exp * CHUNK
    at = iota((1, rows), 1)
    src = sum((at >= CHUNK * m).astype(jnp.int32) for m in range(1, n_exp))
    rest = at - CHUNK * src
    unpack = iota((rows, rows), 0) == rest * n_exp + src
    src = at % n_exp
    pack = iota((rows, rows), 0) == src * CHUNK + at // n_exp
    return unpack, pack


def kernel(
    sizes,
    grad_hbm, ids_hbm, probs_hbm, x_hbm, wg_hbm, wu_hbm, wd_hbm,
    out_ref, prob_out, gate_out, up_out, down_out,
    grad_v, ids_v, probs_v, xb, wg, wu, wd, ids_s, probs_s, prob_all, unpack, pack,
    send_buf, opp_buf, recv_buf, place_t,
    xt, st, slope_up, silu_s, hid_s, hid_r, gate_g, up_g, gate_up, hid_rest, prob_s, own_part,
    xs_opp, xs_left, xs_right, xr1, xr2, ret_send, ret_recv, gather,
    zfirst, zfirst_r, zbuf, zrest,
    load_sem, ysend, yrecv, xsend, xrecv, rsend, rrecv, wsend, wrecv, gsend, grecv, zsend, zrecv,
):
    n_dp, n_exp, n_ten, cap, top, d, hid = sizes
    share = grad_v.shape[1]
    pieces = d // LANES
    group = 2
    groups = n_exp // group
    rest = hid - LANES
    slots = n_exp * cap
    half = slots // 2
    g, q, t = lax.axis_index("dp"), lax.axis_index("expert"), lax.axis_index("tensor")
    t_right, t_left, t_opp = (t + 1) % n_ten, (t + n_ten - 1) % n_ten, (t + 2) % n_ten
    g_right, g_left = (g + 1) % n_dp, (g + n_dp - 1) % n_dp

    def remote(src, dst, send, recv, axis, where):
        return pltpu.make_async_remote_copy(
            src_ref=src, dst_ref=dst, send_sem=send, recv_sem=recv,
            device_id={axis: where}, device_id_type=MESH,
        )

    def tokens_of(tt):
        return pl.ds(pl.multiple_of(tt * share, share), share)

    loads = [
        pltpu.make_async_copy(ids_hbm, ids_v, load_sem.at[0]),
        pltpu.make_async_copy(probs_hbm, probs_v, load_sem.at[1]),
        pltpu.make_async_copy(grad_hbm.at[tokens_of(t)], grad_v.at[0], load_sem.at[2]),
        pltpu.make_async_copy(x_hbm, xb, load_sem.at[3]),
        pltpu.make_async_copy(wg_hbm, wg, load_sem.at[4]),
        pltpu.make_async_copy(wu_hbm, wu, load_sem.at[5]),
        pltpu.make_async_copy(wd_hbm, wd, load_sem.at[6]),
        pltpu.make_async_copy(grad_hbm.at[tokens_of(t_opp)], grad_v.at[1], load_sem.at[7]),
    ]
    for load in loads:
        load.start()
    barrier = pltpu.get_barrier_semaphore()

    def greet(k, carry):
        pl.semaphore_signal(barrier, inc=1, device_id={"expert": (q + k) % n_exp}, device_id_type=MESH)
        return carry

    lax.fori_loop(1, n_exp, greet, 0)
    for axis, where in (("tensor", t_right), ("tensor", t_left), ("dp", g_right), ("dp", g_left)):
        pl.semaphore_signal(barrier, inc=1, device_id={axis: where}, device_id_type=MESH)

    loads[0].wait()
    loads[1].wait()
    fill = jnp.zeros((128 - top, ids_s.shape[0]), F32)
    ids_s[...] = jnp.concatenate([ids_v[...].astype(F32), fill], axis=0).T
    probs_s[...] = jnp.concatenate([probs_v[...], fill], axis=0).T
    lane = iota((share, 128), 1)
    name = (lane * EXP_DEV).astype(F32)
    lower = jnp.where(iota((share, share), 1) < iota((share, share), 0), 1.0, 0.0).astype(BF16)
    spread = ((iota((share, LANES), 1) % share) == iota((share, LANES), 0)).astype(BF16)
    rule = (iota((CHUNK, LANES), 0) - cap * (iota((CHUNK, LANES), 1) // share)).astype(F32)

    def packed(tt, grad):
        ids = ids_s[tokens_of(tt), :]
        probs = probs_s[tokens_of(tt), :]
        routed = jnp.zeros((share, 128), F32)
        prob_tok = jnp.zeros((share, 128), F32)
        for k in range(top):
            hit = ids[:, k : k + 1] == name
            routed = routed + jnp.where(hit, 1.0, 0.0)
            prob_tok = prob_tok + jnp.where(hit, probs[:, k : k + 1], 0.0)
        rank = dot(lower, routed.astype(BF16))
        code = jnp.where(routed > 0.0, rank, -128.0).astype(BF16)
        code_x = dot(code, spread, ((0,), (0,)))
        place = jnp.concatenate(
            [jnp.where(code_x[p : p + 1, :] == rule, 1.0, 0.0).astype(BF16) for p in range(n_exp)], axis=0
        )
        stacked = jnp.concatenate(
            [grad[:, LANES * j : LANES * (j + 1)] for j in range(pieces)]
            + [jnp.concatenate([prob_tok, jnp.zeros((share, LANES - 128), F32)], axis=1).astype(BF16)],
            axis=0,
        )
        return place, dot(place, stacked).astype(BF16).reshape(n_exp, CHUNK, LANES)

    loads[2].wait()
    place, chunks = packed(t, grad_v[0])
    send_buf[...] = chunks
    pl.semaphore_wait(barrier, n_exp + 3)

    mine = q // group
    order = [mine]
    for away in range(1, groups // 2):
        order += [(mine + away) % groups, (mine + groups - away) % groups]
    order.append((mine + groups // 2) % groups)

    def peers(i):
        if i == 0:
            return [order[0] * group + 1 - q % group]
        return [order[i] * group + m for m in range(group)]

    def at_distance(away):
        return [i for i in range(groups) if (i + 1) // 2 == away]

    def ycopy(kind, p):
        src = opp_buf if kind else send_buf
        return remote(src.at[p], recv_buf.at[3 * kind, q], ysend.at[kind, p], yrecv.at[kind, q], "expert", p)

    def ystart(kind, away):
        for i in at_distance(away):
            for p in peers(i):
                ycopy(kind, p).start()

    def yleft(kind, away):
        for i in at_distance(away):
            for p in peers(i):
                ycopy(kind, p).wait_send()

    def ywait(kind, i):
        for p in peers(i):
            remote(
                send_buf.at[p], recv_buf.at[3 * kind, p], ysend.at[kind, p], yrecv.at[kind, p], "expert", p
            ).wait_recv()

    for away in range(3):
        ystart(0, away)
    recv_buf[0, pl.ds(q, 1)] = send_buf[pl.ds(q, 1)]

    def members(i):
        return pl.ds(order[i] * group, group)

    def xcopy(kind, i):
        m = members(i)
        return remote(
            recv_buf.at[0, m], recv_buf.at[1 + kind, m], xsend.at[kind, i], xrecv.at[kind, i],
            "tensor", t_left if kind else t_right,
        )

    def spread_group(i):
        ywait(0, i)
        xcopy(0, i).start()
        xcopy(1, i).start()

    def hand(i):
        left = i % 2
        m = [members(6), members(5), pl.ds(order[7] * group, 1), pl.ds(order[7] * group + 1, 1)][i]
        return remote(
            recv_buf.at[1 + left, m], recv_buf.at[3, m], xsend.at[2, i], xrecv.at[2, i],
            "tensor", t_left if left else t_right,
        )

    def hand_on(i):
        xcopy(i % 2, [6, 5, 7, 7][i]).wait_recv()
        hand(i).start()

    def forward(first, last):
        rows = slice(first, last)
        x = xb[rows, :]
        pre_gate = dot(x, wg[...], nt)
        pre_up = dot(x, wu[...], nt)
        sig = jax.nn.sigmoid(pre_gate)
        silu = pre_gate * sig
        silu_s[rows, :] = silu
        slope_up[rows, :] = pre_up * (sig * (1.0 + pre_gate * (1.0 - sig)))
        hid_s[rows, :] = (silu * pre_up).astype(BF16)

    nt = ((1,), (1,))
    spread_group(0)
    place_t[...] = place.T
    yleft(0, 1)
    ystart(0, 3)
    spread_group(1)
    spread_group(2)
    yleft(0, 2)
    ystart(0, 4)
    loads[7].wait()
    opp_buf[...] = packed(t_opp, grad_v[1])[1]
    ystart(1, 0)
    recv_buf[3, pl.ds(q, 1)] = opp_buf[pl.ds(q, 1)]
    spread_group(3)
    spread_group(4)
    yleft(0, 3)
    ystart(1, 1)
    ystart(1, 2)
    for i in (3, 4, 5):
        loads[i].wait()
    forward(0, 2 * slots)
    opening, closing = unpack_matrices(cap, pieces + 1, n_exp)
    unpack[...] = opening.astype(BF16)
    spread_group(5)
    spread_group(6)
    forward(2 * slots, 4 * slots)
    spread_group(7)
    hand_on(0)
    hand_on(1)
    pack[...] = closing.astype(BF16)
    xt[...] = xb[...].T
    loads[6].wait()

    lane_q = iota((slots, LANES), 1) == q
    blank = 128 - slots

    def rows_of(tt):
        return pl.ds(pl.multiple_of(tt * slots, 32), slots)

    def backward(rel, tt):
        rows = rows_of(tt)
        opened = dot(unpack[...], recv_buf[rel].reshape(n_exp * CHUNK, LANES))

        def piece(j):
            return opened[slots * j : slots * (j + 1), :]

        weight = jnp.sum(jnp.where(lane_q, piece(pieces), 0.0), axis=1, keepdims=True)
        dy = jnp.concatenate([piece(j) for j in range(pieces)], axis=1)
        at = slice(128 * rel, 128 * (rel + 1))
        st[:, at] = jnp.concatenate([(weight * dy).astype(BF16), jnp.zeros((blank, d), BF16)], axis=0).T
        hid_r[at, :] = jnp.concatenate([hid_s[rows, :], jnp.zeros((blank, hid), BF16)], axis=0)
        back = dot(dy.astype(BF16), wd[...], nt)
        prob = jnp.sum(hid_s[rows, :].astype(F32) * back, axis=1, keepdims=True)
        prob_s[rows, :] = jnp.broadcast_to(prob, (slots, 128))
        hidden_grad = weight * back
        gate_g[rows, :] = (hidden_grad * slope_up[rows, :]).astype(BF16)
        up_g[rows, :] = (hidden_grad * silu_s[rows, :]).astype(BF16)

    backward(0, t)
    hand_on(2)
    hand_on(3)
    for i in range(6):
        xcopy(0, i).wait_recv()
    backward(1, t_left)
    for i in (0, 1, 2, 3, 4, 6):
        xcopy(1, i).wait_recv()
    backward(2, t_right)
    for i in range(5):
        ywait(1, i)
    for i in range(4):
        hand(i).wait_recv()
    backward(3, t_opp)
    gate_up[...] = jnp.concatenate([gate_g[:, LANES:], up_g[:, LANES:]], axis=1)
    hid_rest[...] = jnp.concatenate([hid_r[:, LANES:], hid_r[:, LANES:]], axis=1)

    def input_part(tt):
        rows = rows_of(tt)
        return dot(gate_g[rows, :], wg[...]) + dot(up_g[rows, :], wu[...])

    def put_part(ref, tt):
        ref[:, :d] = input_part(tt).astype(BF16)
        ref[:, d:] = prob_s[rows_of(tt), :].astype(BF16)

    lo, hi = pl.ds(0, half), pl.ds(half, half)
    first_right = remote(xs_opp.at[lo], xr1.at[0], rsend.at[0], rrecv.at[0], "tensor", t_right)
    first_left = remote(xs_opp.at[hi], xr1.at[1], rsend.at[1], rrecv.at[1], "tensor", t_left)
    plain_right = remote(xs_right.at[hi], xr2.at[0, hi], rsend.at[2], rrecv.at[2], "tensor", t_right)
    plain_left = remote(xs_left.at[lo], xr2.at[1, lo], rsend.at[3], rrecv.at[3], "tensor", t_left)
    added_right = remote(xs_right.at[lo], xr2.at[0, lo], rsend.at[4], rrecv.at[4], "tensor", t_right)
    added_left = remote(xs_left.at[hi], xr2.at[1, hi], rsend.at[5], rrecv.at[5], "tensor", t_left)

    rows_z = d // n_dp
    hops = n_dp // 2

    fold = rows_z // 2
    first_lanes = iota((fold, 128), 1) < rest

    def zslot(way, sub, s):
        return zrest.at[way, s] if sub == 3 else zbuf.at[way, sub, s]

    def zstart(sub):
        return zfirst_r if sub == 3 else zfirst.at[sub]

    def zcopy(way, sub, s, src):
        return remote(
            src, zslot(way, sub, s), zsend.at[way, sub, s], zrecv.at[way, sub, s], "dp", g_left if way else g_right
        )

    def zrows(way, s):
        owner = (g + hops + s) % n_dp if way else (g + n_dp + hops - s) % n_dp
        return pl.ds(pl.multiple_of(owner * rows_z, 16), rows_z)

    def term(sub, chunks):
        def left(ref):
            return jnp.concatenate([ref[rows, :] for rows in chunks], axis=0)

        if sub < 3:
            right = (gate_g, up_g, hid_r)[sub]
            both = dot(left(st if sub == 2 else xt), right[:, :LANES])
            return [both[rows_z * i : rows_z * (i + 1), :] for i in range(len(chunks))]
        wide_part, narrow = dot(left(xt), gate_up[...]), dot(left(st), hid_rest[...])
        parts = []
        for i in range(len(chunks)):
            at = rows_z * i
            folded = jnp.where(first_lanes, narrow[at : at + fold, :], narrow[at + fold : at + rows_z, :])
            pad = jnp.zeros((zfirst_r.shape[0] - rows_z - fold, 128), F32)
            parts.append(jnp.concatenate([wide_part[at : at + rows_z, :], folded, pad], axis=0))
        return parts

    def zpiece(s, sub, got):
        terms = term(sub, [zrows(0, s), zrows(1, s)])
        for way in range(2):
            total = terms[way]
            slot = zslot(way, sub, s - 1)
            if got[way]:
                zcopy(way, sub, s - 1, slot).wait_recv()
                total = total + slot[...].astype(F32)
            slot[...] = total.astype(BF16)
            zcopy(way, sub, s, slot).start()

    def zsteps(first, end):
        def step(s, carry):
            for sub in range(4):
                zpiece(s, sub, (True, True))
            return carry

        lax.fori_loop(first, end, step, 0)

    for sub in (0, 2, 1, 3):
        zstart(sub)[...] = term(sub, [zrows(0, 0)])[0].astype(BF16)
        zcopy(sub // 2, sub, 0, zstart(sub)).start()
    put_part(xs_opp, t_opp)
    first_right.start()
    first_left.start()

    for sub in range(4):
        zpiece(1, sub, (sub < 2, sub >= 2))
    put_part(xs_right, t_right)
    plain_right.start()
    put_part(xs_left, t_left)
    plain_left.start()
    zsteps(2, 3)
    first_right.wait_recv()
    xs_right[lo, :] = (xs_right[lo, :].astype(F32) + xr1[0].astype(F32)).astype(BF16)
    added_right.start()
    first_left.wait_recv()
    xs_left[hi, :] = (xs_left[hi, :].astype(F32) + xr1[1].astype(F32)).astype(BF16)
    added_left.start()
    own_part[...] = input_part(t)

    zsteps(3, 4)
    for copy in (plain_right, plain_left, added_right, added_left):
        copy.wait_recv()
    slot_input = own_part[...] + xr2[0, :, :d].astype(F32) + xr2[1, :, :d].astype(F32)
    slot_prob = prob_s[rows_of(t), :] + xr2[0, :, d:].astype(F32) + xr2[1, :, d:].astype(F32)
    slot_prob = jnp.where(lane_q, jnp.concatenate([slot_prob] * (LANES // 128), axis=1), 0.0)
    pile = jnp.concatenate(
        [slot_input[:, LANES * j : LANES * (j + 1)] for j in range(pieces)] + [slot_prob], axis=0
    ).astype(BF16)
    ret_send[...] = dot(pack[...], pile).astype(BF16).reshape(n_exp, CHUNK, LANES)

    def partner(i):
        step = i // 2 + 1
        return (q + (i % 2) * (n_exp - 2 * step) + step) % n_exp

    def wcopy(i):
        p = partner(i)
        return remote(ret_send.at[p], ret_recv.at[q], wsend.at[p], wrecv.at[q], "expert", p)

    def wstart(i, carry):
        wcopy(i).start()
        return carry

    lax.fori_loop(0, n_exp - 1, wstart, 0)
    ret_recv[pl.ds(q, 1)] = ret_send[pl.ds(q, 1)]

    zsteps(4, 6)

    def wwait(i, carry):
        p = partner(i)
        remote(ret_send.at[p], ret_recv.at[p], wsend.at[p], wrecv.at[p], "expert", p).wait_recv()
        return carry

    lax.fori_loop(0, n_exp - 1, wwait, 0)
    tokens = dot(place_t[...], ret_recv[...].reshape(n_exp * CHUNK, LANES))
    for j in range(pieces):
        gather[0, :, LANES * j : LANES * (j + 1)] = tokens[share * j : share * (j + 1), :].astype(BF16)
    prob_pos = tokens[share * pieces :, :128]
    prob_tk = jnp.zeros((share, 128), F32)
    ids = ids_s[tokens_of(t), :]
    for k in range(top):
        val = jnp.sum(jnp.where(ids[:, k : k + 1] == name, prob_pos, 0.0), axis=1, keepdims=True)
        prob_tk = jnp.where(lane == k, val, prob_tk)
    gather[0, :, d:] = prob_tk.astype(BF16)

    low, high = pl.ds(0, share // 2), pl.ds(share // 2, share // 2)
    to_right = remote(gather.at[0], gather.at[1], gsend.at[0], grecv.at[0], "tensor", t_right)
    to_left = remote(gather.at[0], gather.at[2], gsend.at[1], grecv.at[1], "tensor", t_left)
    on_right = remote(gather.at[1, low], gather.at[3, low], gsend.at[2], grecv.at[2], "tensor", t_right)
    on_left = remote(gather.at[2, high], gather.at[3, high], gsend.at[3], grecv.at[3], "tensor", t_left)
    to_right.start()
    to_left.start()

    def put_tokens(rel, tt):
        rows = pl.ds(pl.multiple_of(tt * share, share), share)
        out_ref[rows, :] = gather[rel, :, :d]
        prob_all[rows, :] = gather[rel, :, d:].astype(F32)

    put_tokens(0, t)
    zsteps(6, 7)
    to_right.wait_recv()
    on_right.start()
    to_left.wait_recv()
    on_left.start()
    zsteps(7, hops)
    put_tokens(1, t_left)
    put_tokens(2, t_right)
    on_right.wait_recv()
    on_left.wait_recv()
    put_tokens(3, t_opp)

    own = []
    for sub in range(4):
        total = term(sub, [zrows(0, hops)])[0]
        for way in range(2):
            slot = zslot(way, sub, hops - 1)
            zcopy(way, sub, hops - 1, slot).wait_recv()
            total = total + slot[...].astype(F32)
        own.append(total)
    folded = own[3][rows_z : rows_z + fold, :]
    own[3:] = [own[3][:rows_z, :], jnp.concatenate([folded, pltpu.roll(folded, 128 - rest, 1)], axis=0)]
    own = [jnp.concatenate([o, jnp.zeros((128 - rows_z, o.shape[1]), F32)], axis=0).T[:, :rows_z] for o in own]
    gate_out[:LANES, :] = own[0]
    gate_out[LANES:, :] = own[3][:rest]
    up_out[:LANES, :] = own[1]
    up_out[LANES:, :] = own[3][rest : 2 * rest]
    down_out[:LANES, :] = own[2]
    down_out[LANES:, :] = own[4][:rest]
    prob_out[...] = prob_all[...].T[:top]

    def sent(i, carry):
        wcopy(i).wait_send()
        return carry

    lax.fori_loop(0, n_exp - 1, sent, 0)
    for away in (0, 4):
        yleft(0, away)
    for away in range(3):
        yleft(1, away)
    for i in range(groups):
        xcopy(0, i).wait_send()
        xcopy(1, i).wait_send()
    for i in range(4):
        hand(i).wait_send()
    for copy in (first_right, first_left, plain_right, plain_left, added_right, added_left):
        copy.wait_send()
    for copy in (to_right, to_left, on_right, on_left):
        copy.wait_send()

    for sub in range(4):
        zcopy(sub // 2, sub, 0, zstart(sub)).wait_send()

    def zsent(s, carry):
        for way in range(2):
            for sub in range(4):
                zcopy(way, sub, s, zslot(way, sub, s)).wait_send()
        return carry

    lax.fori_loop(1, hops, zsent, 0)


def finish(*refs):
    for src, dst in zip(refs[:5], refs[5:]):
        dst[...] = src[...]


def shards(grad_out, expert_ids, gate_probs, saved_inputs, w_gate, w_up, w_down):
    n_dp, n_exp, n_ten = lax.axis_size("dp"), lax.axis_size("expert"), lax.axis_size("tensor")
    tok_rows, d = grad_out.shape
    cap, top, hid = saved_inputs.shape[4], expert_ids.shape[1], w_gate.shape[2]
    share = tok_rows // n_ten
    slots = n_exp * cap
    total = n_ten * slots
    wide = d + 128
    rows_z = d // n_dp
    rest_rows = rows_z + -(-rows_z // 2 // 16) * 16
    vmem = pltpu.VMEM
    dma = pltpu.SemaphoreType.DMA
    shapes = (
        jax.ShapeDtypeStruct((tok_rows, d), BF16),
        jax.ShapeDtypeStruct((top, tok_rows), F32),
        jax.ShapeDtypeStruct((hid, rows_z), F32),
        jax.ShapeDtypeStruct((hid, rows_z), F32),
        jax.ShapeDtypeStruct((hid, rows_z), F32),
    )
    outs = pl.pallas_call(
        lambda *refs: kernel((n_dp, n_exp, n_ten, cap, top, d, hid), *refs),
        out_shape=shapes,
        in_specs=[pl.BlockSpec(memory_space=pl.ANY)] * 7,
        out_specs=(pl.BlockSpec(memory_space=pltpu.VMEM),) * 5,
        scratch_shapes=[
            vmem((2, share, d), BF16),
            vmem((top, tok_rows), jnp.int32),
            vmem((top, tok_rows), F32),
            vmem((total, d), BF16),
            vmem((hid, d), BF16),
            vmem((hid, d), BF16),
            vmem((hid, d), BF16),
            vmem((tok_rows, 128), F32),
            vmem((tok_rows, 128), F32),
            vmem((tok_rows, 128), F32),
            vmem((n_exp * CHUNK, n_exp * CHUNK), BF16),
            vmem((n_exp * CHUNK, n_exp * CHUNK), BF16),
            vmem((n_exp, CHUNK, LANES), BF16),
            vmem((n_exp, CHUNK, LANES), BF16),
            vmem((4, n_exp, CHUNK, LANES), BF16),
            vmem((LANES, n_exp * CHUNK), BF16),
            vmem((d, total), BF16),
            vmem((d, 4 * 128), BF16),
            vmem((total, hid), F32),
            vmem((total, hid), F32),
            vmem((total, hid), BF16),
            vmem((4 * 128, hid), BF16),
            vmem((total, hid), BF16),
            vmem((total, hid), BF16),
            vmem((total, 128), BF16),
            vmem((4 * 128, 128), BF16),
            vmem((total, 128), F32),
            vmem((slots, d), F32),
            vmem((slots, wide), BF16),
            vmem((slots, wide), BF16),
            vmem((slots, wide), BF16),
            vmem((2, slots // 2, wide), BF16),
            vmem((2, slots, wide), BF16),
            vmem((n_exp, CHUNK, LANES), BF16),
            vmem((n_exp, CHUNK, LANES), BF16),
            vmem((4, share, wide), BF16),
            vmem((3, rows_z, LANES), BF16),
            vmem((rest_rows, 128), BF16),
            vmem((2, 3, n_dp // 2, rows_z, LANES), BF16),
            vmem((2, n_dp // 2, rest_rows, 128), BF16),
            dma((8,)),
            dma((2, n_exp)),
            dma((2, n_exp)),
            dma((3, n_exp // 2)),
            dma((3, n_exp // 2)),
            dma((6,)),
            dma((6,)),
            dma((n_exp,)),
            dma((n_exp,)),
            dma((4,)),
            dma((4,)),
            dma((2, 4, n_dp // 2)),
            dma((2, 4, n_dp // 2)),
        ],
        compiler_params=pltpu.CompilerParams(
            collective_id=0, has_side_effects=True, vmem_limit_bytes=56 * 1024 * 1024
        ),
        name="expert_backward",
    )(
        grad_out,
        expert_ids.T,
        gate_probs.T,
        saved_inputs.transpose(0, 1, 2, 4, 3, 5).reshape(total, d),
        w_gate[0].T,
        w_up[0].T,
        w_down[0].T,
    )
    outs = pl.pallas_call(
        finish,
        out_shape=shapes,
        in_specs=[pl.BlockSpec(memory_space=pltpu.VMEM)] * 5,
        out_specs=(pl.BlockSpec(memory_space=pltpu.VMEM),) * 5,
        name="write_results",
    )(*outs)
    return outs[0], outs[1].T, outs[2].T[None], outs[3].T[None], outs[4].T[None]


def solution(mesh):
    return jax.shard_map(
        shards,
        mesh=mesh,
        in_specs=(
            P(("dp", "expert"), None),
            P(("dp", "expert"), None),
            P(("dp", "expert"), None),
            P("dp", "expert", None, None, None, None),
            P("expert", None, "tensor"),
            P("expert", None, "tensor"),
            P("expert", None, "tensor"),
        ),
        out_specs=(
            P(("dp", "expert"), None),
            P(("dp", "expert"), None),
            P("expert", "dp", "tensor"),
            P("expert", "dp", "tensor"),
            P("expert", "dp", "tensor"),
        ),
        check_vma=False,
    )
```

```python
import jax
import jax.numpy as jnp
from jax import lax
from jax.experimental import pallas as pl
from jax.experimental.pallas import tpu as pltpu
from jax.sharding import PartitionSpec as P

EXP_DEV = 4
LANES = 256
CHUNK = 48
F32 = jnp.float32
BF16 = jnp.bfloat16
MESH = pl.DeviceIdType.MESH


def dot(left, right, dims=((1,), (0,))):
    return lax.dot_general(left, right, (dims, ((), ())), preferred_element_type=F32)


def iota(shape, dim):
    return lax.broadcasted_iota(jnp.int32, shape, dim)


def unpack_matrices(cap, pieces, n_exp):
    rows = n_exp * CHUNK
    at = iota((1, rows), 1)
    src = sum((at >= CHUNK * m).astype(jnp.int32) for m in range(1, n_exp))
    rest = at - CHUNK * src
    unpack = iota((rows, rows), 0) == rest * n_exp + src
    src = at % n_exp
    pack = iota((rows, rows), 0) == src * CHUNK + at // n_exp
    return unpack, pack


def kernel(
    sizes,
    grad_hbm, ids_hbm, probs_hbm, x_hbm, wg_hbm, wu_hbm, wd_hbm,
    out_ref, prob_out, gate_out, up_out, down_out,
    grad_v, ids_v, probs_v, xb, wg, wu, wd, ids_s, probs_s, prob_all, unpack, pack,
    send_buf, opp_buf, recv_buf, place_t,
    xt, st, slope_up, silu_s, hid_s, hid_r, gate_g, up_g, gate_up, hid_rest, prob_s, own_part,
    xs_opp, xs_left, xs_right, xr1, xr2, ret_send, ret_recv, gather,
    zfirst, zfirst_r, zbuf, zrest,
    load_sem, ysend, yrecv, xsend, xrecv, rsend, rrecv, wsend, wrecv, gsend, grecv, zsend, zrecv,
):
    n_dp, n_exp, n_ten, cap, top, d, hid = sizes
    share = grad_v.shape[1]
    pieces = d // LANES
    group = 2
    groups = n_exp // group
    rest = hid - LANES
    slots = n_exp * cap
    half = slots // 2
    g, q, t = lax.axis_index("dp"), lax.axis_index("expert"), lax.axis_index("tensor")
    t_right, t_left, t_opp = (t + 1) % n_ten, (t + n_ten - 1) % n_ten, (t + 2) % n_ten
    g_right, g_left = (g + 1) % n_dp, (g + n_dp - 1) % n_dp

    def remote(src, dst, send, recv, axis, where):
        return pltpu.make_async_remote_copy(
            src_ref=src, dst_ref=dst, send_sem=send, recv_sem=recv,
            device_id={axis: where}, device_id_type=MESH,
        )

    def tokens_of(tt):
        return pl.ds(pl.multiple_of(tt * share, share), share)

    loads = [
        pltpu.make_async_copy(ids_hbm, ids_v, load_sem.at[0]),
        pltpu.make_async_copy(probs_hbm, probs_v, load_sem.at[1]),
        pltpu.make_async_copy(grad_hbm.at[tokens_of(t)], grad_v.at[0], load_sem.at[2]),
        pltpu.make_async_copy(x_hbm, xb, load_sem.at[3]),
        pltpu.make_async_copy(wg_hbm, wg, load_sem.at[4]),
        pltpu.make_async_copy(wu_hbm, wu, load_sem.at[5]),
        pltpu.make_async_copy(wd_hbm, wd, load_sem.at[6]),
        pltpu.make_async_copy(grad_hbm.at[tokens_of(t_opp)], grad_v.at[1], load_sem.at[7]),
    ]
    for load in loads:
        load.start()
    barrier = pltpu.get_barrier_semaphore()

    def greet(k, carry):
        pl.semaphore_signal(barrier, inc=1, device_id={"expert": (q + k) % n_exp}, device_id_type=MESH)
        return carry

    lax.fori_loop(1, n_exp, greet, 0)
    for axis, where in (("tensor", t_right), ("tensor", t_left), ("dp", g_right), ("dp", g_left)):
        pl.semaphore_signal(barrier, inc=1, device_id={axis: where}, device_id_type=MESH)

    loads[0].wait()
    loads[1].wait()
    fill = jnp.zeros((128 - top, ids_s.shape[0]), F32)
    ids_s[...] = jnp.concatenate([ids_v[...].astype(F32), fill], axis=0).T
    probs_s[...] = jnp.concatenate([probs_v[...], fill], axis=0).T
    lane = iota((share, 128), 1)
    name = (lane * EXP_DEV).astype(F32)
    lower = jnp.where(iota((share, share), 1) < iota((share, share), 0), 1.0, 0.0).astype(BF16)
    spread = ((iota((share, LANES), 1) % share) == iota((share, LANES), 0)).astype(BF16)
    rule = (iota((CHUNK, LANES), 0) - cap * (iota((CHUNK, LANES), 1) // share)).astype(F32)

    def packed(tt, grad):
        ids = ids_s[tokens_of(tt), :]
        probs = probs_s[tokens_of(tt), :]
        routed = jnp.zeros((share, 128), F32)
        prob_tok = jnp.zeros((share, 128), F32)
        for k in range(top):
            hit = ids[:, k : k + 1] == name
            routed = routed + jnp.where(hit, 1.0, 0.0)
            prob_tok = prob_tok + jnp.where(hit, probs[:, k : k + 1], 0.0)
        rank = dot(lower, routed.astype(BF16))
        code = jnp.where(routed > 0.0, rank, -128.0).astype(BF16)
        code_x = dot(code, spread, ((0,), (0,)))
        place = jnp.concatenate(
            [jnp.where(code_x[p : p + 1, :] == rule, 1.0, 0.0).astype(BF16) for p in range(n_exp)], axis=0
        )
        stacked = jnp.concatenate(
            [grad[:, LANES * j : LANES * (j + 1)] for j in range(pieces)]
            + [jnp.concatenate([prob_tok, jnp.zeros((share, LANES - 128), F32)], axis=1).astype(BF16)],
            axis=0,
        )
        return place, dot(place, stacked).astype(BF16).reshape(n_exp, CHUNK, LANES)

    loads[2].wait()
    place, chunks = packed(t, grad_v[0])
    send_buf[...] = chunks
    pl.semaphore_wait(barrier, n_exp + 3)

    mine = q // group
    order = [mine]
    for away in range(1, groups // 2):
        order += [(mine + away) % groups, (mine + groups - away) % groups]
    order.append((mine + groups // 2) % groups)

    def peers(i):
        if i == 0:
            return [order[0] * group + 1 - q % group]
        return [order[i] * group + m for m in range(group)]

    def at_distance(away):
        return [i for i in range(groups) if (i + 1) // 2 == away]

    def ycopy(kind, p):
        src = opp_buf if kind else send_buf
        return remote(src.at[p], recv_buf.at[3 * kind, q], ysend.at[kind, p], yrecv.at[kind, q], "expert", p)

    def ystart(kind, away):
        for i in at_distance(away):
            for p in peers(i):
                ycopy(kind, p).start()

    def yleft(kind, away):
        for i in at_distance(away):
            for p in peers(i):
                ycopy(kind, p).wait_send()

    def ywait(kind, i):
        for p in peers(i):
            remote(
                send_buf.at[p], recv_buf.at[3 * kind, p], ysend.at[kind, p], yrecv.at[kind, p], "expert", p
            ).wait_recv()

    for away in range(3):
        ystart(0, away)
    recv_buf[0, pl.ds(q, 1)] = send_buf[pl.ds(q, 1)]

    def members(i):
        return pl.ds(order[i] * group, group)

    def xcopy(kind, i):
        m = members(i)
        return remote(
            recv_buf.at[0, m], recv_buf.at[1 + kind, m], xsend.at[kind, i], xrecv.at[kind, i],
            "tensor", t_left if kind else t_right,
        )

    def spread_group(i):
        ywait(0, i)
        xcopy(0, i).start()
        xcopy(1, i).start()

    handed = [6, 5, 7, 7]
    extra = (0, 1, 2)

    def hand(i):
        left = i % 2
        m = [members(6), members(5), pl.ds(order[7] * group, 1), pl.ds(order[7] * group + 1, 1)][i]
        return remote(
            recv_buf.at[1 + left, m], recv_buf.at[3, m], xsend.at[2, i], xrecv.at[2, i],
            "tensor", t_left if left else t_right,
        )

    def hand_on(i):
        xcopy(i % 2, handed[i]).wait_recv()
        hand(i).start()

    def forward(first, last):
        rows = slice(first, last)
        x = xb[rows, :]
        pre_gate = dot(x, wg[...], nt)
        pre_up = dot(x, wu[...], nt)
        sig = jax.nn.sigmoid(pre_gate)
        silu = pre_gate * sig
        silu_s[rows, :] = silu
        slope_up[rows, :] = pre_up * (sig * (1.0 + pre_gate * (1.0 - sig)))
        hid_s[rows, :] = (silu * pre_up).astype(BF16)

    nt = ((1,), (1,))
    spread_group(0)
    place_t[...] = place.T
    yleft(0, 1)
    ystart(0, 3)
    spread_group(1)
    spread_group(2)
    yleft(0, 2)
    ystart(0, 4)
    loads[7].wait()
    opp_buf[...] = packed(t_opp, grad_v[1])[1]
    ystart(1, 0)
    recv_buf[3, pl.ds(q, 1)] = opp_buf[pl.ds(q, 1)]
    spread_group(3)
    spread_group(4)
    yleft(0, 3)
    ystart(1, 1)
    ystart(1, 2)
    for i in (3, 4, 5):
        loads[i].wait()
    forward(0, 2 * slots)
    opening, closing = unpack_matrices(cap, pieces + 1, n_exp)
    unpack[...] = opening.astype(BF16)
    spread_group(5)
    spread_group(6)
    forward(2 * slots, 4 * slots)
    spread_group(7)
    hand_on(0)
    hand_on(1)
    pack[...] = closing.astype(BF16)
    xt[...] = xb[...].T
    loads[6].wait()

    lane_q = iota((slots, LANES), 1) == q
    blank = 128 - slots

    def rows_of(tt):
        return pl.ds(pl.multiple_of(tt * slots, 32), slots)

    rows_z = d // n_dp
    hops = n_dp // 2

    fold = rows_z // 2
    first_lanes = iota((fold, 128), 1) < rest

    def zslot(way, sub, s):
        return zrest.at[way, s] if sub == 3 else zbuf.at[way, sub, s]

    def zstart(sub):
        return zfirst_r if sub == 3 else zfirst.at[sub]

    def zcopy(way, sub, s, src):
        return remote(
            src, zslot(way, sub, s), zsend.at[way, sub, s], zrecv.at[way, sub, s], "dp", g_left if way else g_right
        )

    def zrows(way, s):
        owner = (g + hops + s) % n_dp if way else (g + n_dp + hops - s) % n_dp
        return pl.ds(pl.multiple_of(owner * rows_z, 16), rows_z)

    def term(sub, chunks):
        def left(ref):
            return jnp.concatenate([ref[rows, :] for rows in chunks], axis=0)

        if sub < 3:
            right = (gate_g, up_g, hid_r)[sub]
            both = dot(left(st if sub == 2 else xt), right[:, :LANES])
            return [both[rows_z * i : rows_z * (i + 1), :] for i in range(len(chunks))]
        wide_part, narrow = dot(left(xt), gate_up[...]), dot(left(st), hid_rest[...])
        parts = []
        for i in range(len(chunks)):
            at = rows_z * i
            folded = jnp.where(first_lanes, narrow[at : at + fold, :], narrow[at + fold : at + rows_z, :])
            pad = jnp.zeros((zfirst_r.shape[0] - rows_z - fold, 128), F32)
            parts.append(jnp.concatenate([wide_part[at : at + rows_z, :], folded, pad], axis=0))
        return parts

    def zpiece(s, sub):
        terms = term(sub, [zrows(0, s), zrows(1, s)])
        for way in range(2):
            total = terms[way]
            slot = zslot(way, sub, s - 1)
            zcopy(way, sub, s - 1, slot).wait_recv()
            slot[...] = (total + slot[...].astype(F32)).astype(BF16)
            zcopy(way, sub, s, slot).start()

    def zsteps(first, end):
        def step(s, carry):
            for sub in range(4):
                zpiece(s, sub)
            return carry

        lax.fori_loop(first, end, step, 0)

    def zfirst_pair(sub):
        way = sub % 2
        begin, later = term(sub, [zrows(way, 0), zrows(1 - way, 1)])
        zstart(sub)[...] = begin.astype(BF16)
        zcopy(way, sub, 0, zstart(sub)).start()
        slot = zslot(1 - way, sub, 0)
        slot[...] = later.astype(BF16)
        zcopy(1 - way, sub, 1, slot).start()

    def zsecond(sub):
        way = sub % 2
        slot = zslot(way, sub, 0)
        total = term(sub, [zrows(way, 1)])[0]
        zcopy(way, sub, 0, slot).wait_recv()
        slot[...] = (total + slot[...].astype(F32)).astype(BF16)
        zcopy(way, sub, 1, slot).start()

    def opened_block(rel, tt):
        rows = rows_of(tt)
        opened = dot(unpack[...], recv_buf[rel].reshape(n_exp * CHUNK, LANES))

        def piece(j):
            return opened[slots * j : slots * (j + 1), :]

        weight = jnp.sum(jnp.where(lane_q, piece(pieces), 0.0), axis=1, keepdims=True)
        dy = jnp.concatenate([piece(j) for j in range(pieces)], axis=1)
        at = slice(128 * rel, 128 * (rel + 1))
        st[:, at] = jnp.concatenate([(weight * dy).astype(BF16), jnp.zeros((blank, d), BF16)], axis=0).T
        hid_r[at, :] = jnp.concatenate([hid_s[rows, :], jnp.zeros((blank, hid), BF16)], axis=0)

        def hidden_part():
            finish_block(rows, dy.astype(BF16), weight)

        return hidden_part

    def finish_block(rows, dy, weight):
        back = dot(dy, wd[...], nt)
        prob = jnp.sum(hid_s[rows, :].astype(F32) * back, axis=1, keepdims=True)
        prob_s[rows, :] = jnp.broadcast_to(prob, (slots, 128))
        hidden_grad = weight * back
        gate_g[rows, :] = (hidden_grad * slope_up[rows, :]).astype(BF16)
        up_g[rows, :] = (hidden_grad * silu_s[rows, :]).astype(BF16)

    def backward(rel, tt):
        opened_block(rel, tt)()

    backward(0, t)
    hand_on(2)
    hand_on(3)
    for i in range(6):
        xcopy(0, i).wait_recv()
    backward(1, t_left)
    for i in (0, 1, 2, 3, 4, 6):
        xcopy(1, i).wait_recv()
    backward(2, t_right)
    for away in extra:
        for i in at_distance(away):
            ywait(1, i)
    for i in range(4):
        hand(i).wait_recv()
    hidden_part = opened_block(3, t_opp)
    zfirst_pair(2)
    hidden_part()
    gate_up[...] = jnp.concatenate([gate_g[:, LANES:], up_g[:, LANES:]], axis=1)
    hid_rest[...] = jnp.concatenate([hid_r[:, LANES:], hid_r[:, LANES:]], axis=1)

    def input_part(tt):
        rows = rows_of(tt)
        return dot(gate_g[rows, :], wg[...]) + dot(up_g[rows, :], wu[...])

    def put_part(ref, tt):
        ref[:, :d] = input_part(tt).astype(BF16)
        ref[:, d:] = prob_s[rows_of(tt), :].astype(BF16)

    lo, hi = pl.ds(0, half), pl.ds(half, half)
    first_right = remote(xs_opp.at[lo], xr1.at[0], rsend.at[0], rrecv.at[0], "tensor", t_right)
    first_left = remote(xs_opp.at[hi], xr1.at[1], rsend.at[1], rrecv.at[1], "tensor", t_left)
    plain_right = remote(xs_right.at[hi], xr2.at[0, hi], rsend.at[2], rrecv.at[2], "tensor", t_right)
    plain_left = remote(xs_left.at[lo], xr2.at[1, lo], rsend.at[3], rrecv.at[3], "tensor", t_left)
    added_right = remote(xs_right.at[lo], xr2.at[0, lo], rsend.at[4], rrecv.at[4], "tensor", t_right)
    added_left = remote(xs_left.at[hi], xr2.at[1, hi], rsend.at[5], rrecv.at[5], "tensor", t_left)

    for sub in (1, 0, 3):
        zfirst_pair(sub)
    put_part(xs_opp, t_opp)
    first_right.start()
    first_left.start()

    for sub in (2, 1, 0, 3):
        zsecond(sub)
    put_part(xs_right, t_right)
    plain_right.start()
    put_part(xs_left, t_left)
    plain_left.start()
    zsteps(2, 3)
    first_right.wait_recv()
    xs_right[lo, :] = (xs_right[lo, :].astype(F32) + xr1[0].astype(F32)).astype(BF16)
    added_right.start()
    first_left.wait_recv()
    xs_left[hi, :] = (xs_left[hi, :].astype(F32) + xr1[1].astype(F32)).astype(BF16)
    added_left.start()
    own_part[...] = input_part(t)

    zsteps(3, 4)
    for copy in (plain_right, plain_left, added_right, added_left):
        copy.wait_recv()
    slot_input = own_part[...] + xr2[0, :, :d].astype(F32) + xr2[1, :, :d].astype(F32)
    slot_prob = prob_s[rows_of(t), :] + xr2[0, :, d:].astype(F32) + xr2[1, :, d:].astype(F32)
    slot_prob = jnp.where(lane_q, jnp.concatenate([slot_prob] * (LANES // 128), axis=1), 0.0)
    pile = jnp.concatenate(
        [slot_input[:, LANES * j : LANES * (j + 1)] for j in range(pieces)] + [slot_prob], axis=0
    ).astype(BF16)
    ret_send[...] = dot(pack[...], pile).astype(BF16).reshape(n_exp, CHUNK, LANES)

    def partner(i):
        step = i // 2 + 1
        return (q + (i % 2) * (n_exp - 2 * step) + step) % n_exp

    def wcopy(i):
        p = partner(i)
        return remote(ret_send.at[p], ret_recv.at[q], wsend.at[p], wrecv.at[q], "expert", p)

    def wstart(i, carry):
        wcopy(i).start()
        return carry

    lax.fori_loop(0, n_exp - 1, wstart, 0)
    ret_recv[pl.ds(q, 1)] = ret_send[pl.ds(q, 1)]

    zsteps(4, 6)

    def wwait(i, carry):
        p = partner(i)
        remote(ret_send.at[p], ret_recv.at[p], wsend.at[p], wrecv.at[p], "expert", p).wait_recv()
        return carry

    lax.fori_loop(0, n_exp - 1, wwait, 0)
    tokens = dot(place_t[...], ret_recv[...].reshape(n_exp * CHUNK, LANES))
    for j in range(pieces):
        gather[0, :, LANES * j : LANES * (j + 1)] = tokens[share * j : share * (j + 1), :].astype(BF16)
    prob_pos = tokens[share * pieces :, :128]
    prob_tk = jnp.zeros((share, 128), F32)
    ids = ids_s[tokens_of(t), :]
    for k in range(top):
        val = jnp.sum(jnp.where(ids[:, k : k + 1] == name, prob_pos, 0.0), axis=1, keepdims=True)
        prob_tk = jnp.where(lane == k, val, prob_tk)
    gather[0, :, d:] = prob_tk.astype(BF16)

    low, high = pl.ds(0, share // 2), pl.ds(share // 2, share // 2)
    to_right = remote(gather.at[0], gather.at[1], gsend.at[0], grecv.at[0], "tensor", t_right)
    to_left = remote(gather.at[0], gather.at[2], gsend.at[1], grecv.at[1], "tensor", t_left)
    on_right = remote(gather.at[1, low], gather.at[3, low], gsend.at[2], grecv.at[2], "tensor", t_right)
    on_left = remote(gather.at[2, high], gather.at[3, high], gsend.at[3], grecv.at[3], "tensor", t_left)
    to_right.start()
    to_left.start()

    def put_tokens(rel, tt):
        rows = pl.ds(pl.multiple_of(tt * share, share), share)
        out_ref[rows, :] = gather[rel, :, :d]
        prob_all[rows, :] = gather[rel, :, d:].astype(F32)

    put_tokens(0, t)
    zsteps(6, 7)
    to_right.wait_recv()
    on_right.start()
    to_left.wait_recv()
    on_left.start()
    zsteps(7, hops)
    put_tokens(1, t_left)
    put_tokens(2, t_right)
    on_right.wait_recv()
    on_left.wait_recv()
    put_tokens(3, t_opp)

    own = []
    for sub in range(4):
        total = term(sub, [zrows(0, hops)])[0]
        for way in range(2):
            slot = zslot(way, sub, hops - 1)
            zcopy(way, sub, hops - 1, slot).wait_recv()
            total = total + slot[...].astype(F32)
        own.append(total)
    folded = own[3][rows_z : rows_z + fold, :]
    own[3:] = [own[3][:rows_z, :], jnp.concatenate([folded, pltpu.roll(folded, 128 - rest, 1)], axis=0)]
    own = [jnp.concatenate([o, jnp.zeros((128 - rows_z, o.shape[1]), F32)], axis=0).T[:, :rows_z] for o in own]
    gate_out[:LANES, :] = own[0]
    gate_out[LANES:, :] = own[3][:rest]
    up_out[:LANES, :] = own[1]
    up_out[LANES:, :] = own[3][rest : 2 * rest]
    down_out[:LANES, :] = own[2]
    down_out[LANES:, :] = own[4][:rest]
    prob_out[...] = prob_all[...].T[:top]

    def sent(i, carry):
        wcopy(i).wait_send()
        return carry

    lax.fori_loop(0, n_exp - 1, sent, 0)
    for away in (0, 4):
        yleft(0, away)
    for away in extra:
        yleft(1, away)
    for i in range(groups):
        xcopy(0, i).wait_send()
        xcopy(1, i).wait_send()
    for i in range(4):
        hand(i).wait_send()
    for copy in (first_right, first_left, plain_right, plain_left, added_right, added_left):
        copy.wait_send()
    for copy in (to_right, to_left, on_right, on_left):
        copy.wait_send()

    for sub in range(4):
        zcopy(sub % 2, sub, 0, zstart(sub)).wait_send()

    def zsent(s, carry):
        for way in range(2):
            for sub in range(4):
                zcopy(way, sub, s, zslot(way, sub, s)).wait_send()
        return carry

    lax.fori_loop(1, hops, zsent, 0)


def finish(*refs):
    for src, dst in zip(refs[:5], refs[5:]):
        dst[...] = src[...]


def shards(grad_out, expert_ids, gate_probs, saved_inputs, w_gate, w_up, w_down):
    n_dp, n_exp, n_ten = lax.axis_size("dp"), lax.axis_size("expert"), lax.axis_size("tensor")
    tok_rows, d = grad_out.shape
    cap, top, hid = saved_inputs.shape[4], expert_ids.shape[1], w_gate.shape[2]
    share = tok_rows // n_ten
    slots = n_exp * cap
    total = n_ten * slots
    wide = d + 128
    rows_z = d // n_dp
    rest_rows = rows_z + -(-rows_z // 2 // 16) * 16
    vmem = pltpu.VMEM
    dma = pltpu.SemaphoreType.DMA
    shapes = (
        jax.ShapeDtypeStruct((tok_rows, d), BF16),
        jax.ShapeDtypeStruct((top, tok_rows), F32),
        jax.ShapeDtypeStruct((hid, rows_z), F32),
        jax.ShapeDtypeStruct((hid, rows_z), F32),
        jax.ShapeDtypeStruct((hid, rows_z), F32),
    )
    outs = pl.pallas_call(
        lambda *refs: kernel((n_dp, n_exp, n_ten, cap, top, d, hid), *refs),
        out_shape=shapes,
        in_specs=[pl.BlockSpec(memory_space=pl.ANY)] * 7,
        out_specs=(pl.BlockSpec(memory_space=pltpu.VMEM),) * 5,
        scratch_shapes=[
            vmem((2, share, d), BF16),
            vmem((top, tok_rows), jnp.int32),
            vmem((top, tok_rows), F32),
            vmem((total, d), BF16),
            vmem((hid, d), BF16),
            vmem((hid, d), BF16),
            vmem((hid, d), BF16),
            vmem((tok_rows, 128), F32),
            vmem((tok_rows, 128), F32),
            vmem((tok_rows, 128), F32),
            vmem((n_exp * CHUNK, n_exp * CHUNK), BF16),
            vmem((n_exp * CHUNK, n_exp * CHUNK), BF16),
            vmem((n_exp, CHUNK, LANES), BF16),
            vmem((n_exp, CHUNK, LANES), BF16),
            vmem((4, n_exp, CHUNK, LANES), BF16),
            vmem((LANES, n_exp * CHUNK), BF16),
            vmem((d, total), BF16),
            vmem((d, 4 * 128), BF16),
            vmem((total, hid), F32),
            vmem((total, hid), F32),
            vmem((total, hid), BF16),
            vmem((4 * 128, hid), BF16),
            vmem((total, hid), BF16),
            vmem((total, hid), BF16),
            vmem((total, 128), BF16),
            vmem((4 * 128, 128), BF16),
            vmem((total, 128), F32),
            vmem((slots, d), F32),
            vmem((slots, wide), BF16),
            vmem((slots, wide), BF16),
            vmem((slots, wide), BF16),
            vmem((2, slots // 2, wide), BF16),
            vmem((2, slots, wide), BF16),
            vmem((n_exp, CHUNK, LANES), BF16),
            vmem((n_exp, CHUNK, LANES), BF16),
            vmem((4, share, wide), BF16),
            vmem((3, rows_z, LANES), BF16),
            vmem((rest_rows, 128), BF16),
            vmem((2, 3, n_dp // 2, rows_z, LANES), BF16),
            vmem((2, n_dp // 2, rest_rows, 128), BF16),
            dma((8,)),
            dma((2, n_exp)),
            dma((2, n_exp)),
            dma((3, n_exp // 2)),
            dma((3, n_exp // 2)),
            dma((6,)),
            dma((6,)),
            dma((n_exp,)),
            dma((n_exp,)),
            dma((4,)),
            dma((4,)),
            dma((2, 4, n_dp // 2)),
            dma((2, 4, n_dp // 2)),
        ],
        compiler_params=pltpu.CompilerParams(
            collective_id=0, has_side_effects=True, vmem_limit_bytes=56 * 1024 * 1024
        ),
        name="expert_backward",
    )(
        grad_out,
        expert_ids.T,
        gate_probs.T,
        saved_inputs.transpose(0, 1, 2, 4, 3, 5).reshape(total, d),
        w_gate[0].T,
        w_up[0].T,
        w_down[0].T,
    )
    outs = pl.pallas_call(
        finish,
        out_shape=shapes,
        in_specs=[pl.BlockSpec(memory_space=pltpu.VMEM)] * 5,
        out_specs=(pl.BlockSpec(memory_space=pltpu.VMEM),) * 5,
        name="write_results",
    )(*outs)
    return outs[0], outs[1].T, outs[2].T[None], outs[3].T[None], outs[4].T[None]


def solution(mesh):
    return jax.shard_map(
        shards,
        mesh=mesh,
        in_specs=(
            P(("dp", "expert"), None),
            P(("dp", "expert"), None),
            P(("dp", "expert"), None),
            P("dp", "expert", None, None, None, None),
            P("expert", None, "tensor"),
            P("expert", None, "tensor"),
            P("expert", None, "tensor"),
        ),
        out_specs=(
            P(("dp", "expert"), None),
            P(("dp", "expert"), None),
            P("expert", "dp", "tensor"),
            P("expert", "dp", "tensor"),
            P("expert", "dp", "tensor"),
        ),
        check_vma=False,
    )
```

```python
import jax
import jax.numpy as jnp
from jax import lax
from jax.experimental import pallas as pl
from jax.experimental.pallas import tpu as pltpu
from jax.sharding import PartitionSpec as P

EXP_DEV = 4
LANES = 256
CHUNK = 48
F32 = jnp.float32
BF16 = jnp.bfloat16
MESH = pl.DeviceIdType.MESH


def dot(left, right, dims=((1,), (0,))):
    return lax.dot_general(left, right, (dims, ((), ())), preferred_element_type=F32)


def iota(shape, dim):
    return lax.broadcasted_iota(jnp.int32, shape, dim)


def unpack_matrices(cap, pieces, n_exp):
    rows = n_exp * CHUNK
    at = iota((1, rows), 1)
    src = sum((at >= CHUNK * m).astype(jnp.int32) for m in range(1, n_exp))
    rest = at - CHUNK * src
    unpack = iota((rows, rows), 0) == rest * n_exp + src
    src = at % n_exp
    pack = iota((rows, rows), 0) == src * CHUNK + at // n_exp
    return unpack, pack


def kernel(
    sizes,
    grad_hbm, ids_hbm, probs_hbm, x_hbm, wg_hbm, wu_hbm, wd_hbm,
    out_ref, prob_out, gate_out, up_out, down_out,
    grad_v, ids_v, probs_v, xb, wg, wu, wd, ids_s, probs_s, prob_all, unpack, pack,
    send_buf, opp_buf, recv_buf, place_t,
    xt, st, slope_up, silu_s, hid_s, hid_r, gate_g, up_g, gate_up, hid_rest, prob_s, own_part,
    xs_opp, xs_left, xs_right, xr1, xr2, ret_send, ret_recv, gather,
    zfirst, zfirst_r, zbuf, zrest,
    load_sem, ysend, yrecv, xsend, xrecv, rsend, rrecv, wsend, wrecv, gsend, grecv, zsend, zrecv,
):
    n_dp, n_exp, n_ten, cap, top, d, hid = sizes
    share = grad_v.shape[1]
    pieces = d // LANES
    group = 2
    groups = n_exp // group
    rest = hid - LANES
    slots = n_exp * cap
    half = slots // 2
    g, q, t = lax.axis_index("dp"), lax.axis_index("expert"), lax.axis_index("tensor")
    t_right, t_left, t_opp = (t + 1) % n_ten, (t + n_ten - 1) % n_ten, (t + 2) % n_ten
    g_right, g_left = (g + 1) % n_dp, (g + n_dp - 1) % n_dp

    def remote(src, dst, send, recv, axis, where):
        return pltpu.make_async_remote_copy(
            src_ref=src, dst_ref=dst, send_sem=send, recv_sem=recv,
            device_id={axis: where}, device_id_type=MESH,
        )

    def tokens_of(tt):
        return pl.ds(pl.multiple_of(tt * share, share), share)

    loads = [
        pltpu.make_async_copy(ids_hbm, ids_v, load_sem.at[0]),
        pltpu.make_async_copy(probs_hbm, probs_v, load_sem.at[1]),
        pltpu.make_async_copy(grad_hbm.at[tokens_of(t)], grad_v.at[0], load_sem.at[2]),
        pltpu.make_async_copy(x_hbm, xb, load_sem.at[3]),
        pltpu.make_async_copy(wg_hbm, wg, load_sem.at[4]),
        pltpu.make_async_copy(wu_hbm, wu, load_sem.at[5]),
        pltpu.make_async_copy(wd_hbm, wd, load_sem.at[6]),
        pltpu.make_async_copy(grad_hbm.at[tokens_of(t_opp)], grad_v.at[1], load_sem.at[7]),
    ]
    for load in loads:
        load.start()
    barrier = pltpu.get_barrier_semaphore()

    def greet(k, carry):
        pl.semaphore_signal(barrier, inc=1, device_id={"expert": (q + k) % n_exp}, device_id_type=MESH)
        return carry

    lax.fori_loop(1, n_exp, greet, 0)
    for axis, where in (("tensor", t_right), ("tensor", t_left), ("dp", g_right), ("dp", g_left)):
        pl.semaphore_signal(barrier, inc=1, device_id={axis: where}, device_id_type=MESH)

    loads[0].wait()
    loads[1].wait()
    fill = jnp.zeros((128 - top, ids_s.shape[0]), F32)
    ids_s[...] = jnp.concatenate([ids_v[...].astype(F32), fill], axis=0).T
    probs_s[...] = jnp.concatenate([probs_v[...], fill], axis=0).T
    lane = iota((share, 128), 1)
    name = (lane * EXP_DEV).astype(F32)
    lower = jnp.where(iota((share, share), 1) < iota((share, share), 0), 1.0, 0.0).astype(BF16)
    spread = ((iota((share, LANES), 1) % share) == iota((share, LANES), 0)).astype(BF16)
    rule = (iota((CHUNK, LANES), 0) - cap * (iota((CHUNK, LANES), 1) // share)).astype(F32)

    def packed(tt, grad):
        ids = ids_s[tokens_of(tt), :]
        probs = probs_s[tokens_of(tt), :]
        routed = jnp.zeros((share, 128), F32)
        prob_tok = jnp.zeros((share, 128), F32)
        for k in range(top):
            hit = ids[:, k : k + 1] == name
            routed = routed + jnp.where(hit, 1.0, 0.0)
            prob_tok = prob_tok + jnp.where(hit, probs[:, k : k + 1], 0.0)
        rank = dot(lower, routed.astype(BF16))
        code = jnp.where(routed > 0.0, rank, -128.0).astype(BF16)
        code_x = dot(code, spread, ((0,), (0,)))
        place = jnp.concatenate(
            [jnp.where(code_x[p : p + 1, :] == rule, 1.0, 0.0).astype(BF16) for p in range(n_exp)], axis=0
        )
        stacked = jnp.concatenate(
            [grad[:, LANES * j : LANES * (j + 1)] for j in range(pieces)]
            + [jnp.concatenate([prob_tok, jnp.zeros((share, LANES - 128), F32)], axis=1).astype(BF16)],
            axis=0,
        )
        return place, dot(place, stacked).astype(BF16).reshape(n_exp, CHUNK, LANES)

    loads[2].wait()
    place, chunks = packed(t, grad_v[0])
    send_buf[...] = chunks
    pl.semaphore_wait(barrier, n_exp + 3)

    mine = q // group
    order = [mine]
    for away in range(1, groups // 2):
        order += [(mine + away) % groups, (mine + groups - away) % groups]
    order.append((mine + groups // 2) % groups)

    def peers(i):
        if i == 0:
            return [order[0] * group + 1 - q % group]
        return [order[i] * group + m for m in range(group)]

    def at_distance(away):
        return [i for i in range(groups) if (i + 1) // 2 == away]

    def ycopy(kind, p):
        src = opp_buf if kind else send_buf
        return remote(src.at[p], recv_buf.at[3 * kind, q], ysend.at[kind, p], yrecv.at[kind, q], "expert", p)

    def ystart(kind, away):
        for i in at_distance(away):
            for p in peers(i):
                ycopy(kind, p).start()

    def yleft(kind, away):
        for i in at_distance(away):
            for p in peers(i):
                ycopy(kind, p).wait_send()

    def ywait(kind, i):
        for p in peers(i):
            remote(
                send_buf.at[p], recv_buf.at[3 * kind, p], ysend.at[kind, p], yrecv.at[kind, p], "expert", p
            ).wait_recv()

    for away in range(3):
        ystart(0, away)
    recv_buf[0, pl.ds(q, 1)] = send_buf[pl.ds(q, 1)]

    def members(i):
        return pl.ds(order[i] * group, group)

    def xcopy(kind, i):
        m = members(i)
        return remote(
            recv_buf.at[0, m], recv_buf.at[1 + kind, m], xsend.at[kind, i], xrecv.at[kind, i],
            "tensor", t_left if kind else t_right,
        )

    def spread_group(i):
        ywait(0, i)
        xcopy(0, i).start()
        xcopy(1, i).start()

    handed = [6, 5, 7, 7]
    extra = (0, 1, 2)

    def hand(i):
        left = i % 2
        m = [members(6), members(5), pl.ds(order[7] * group, 1), pl.ds(order[7] * group + 1, 1)][i]
        return remote(
            recv_buf.at[1 + left, m], recv_buf.at[3, m], xsend.at[2, i], xrecv.at[2, i],
            "tensor", t_left if left else t_right,
        )

    def hand_on(i):
        xcopy(i % 2, handed[i]).wait_recv()
        hand(i).start()

    def forward(first, last):
        rows = slice(first, last)
        x = xb[rows, :]
        pre_gate = dot(x, wg[...], nt)
        pre_up = dot(x, wu[...], nt)
        sig = jax.nn.sigmoid(pre_gate)
        silu = pre_gate * sig
        silu_s[rows, :] = silu
        slope_up[rows, :] = pre_up * (sig * (1.0 + pre_gate * (1.0 - sig)))
        hid_s[rows, :] = (silu * pre_up).astype(BF16)

    nt = ((1,), (1,))
    spread_group(0)
    place_t[...] = place.T
    yleft(0, 1)
    ystart(0, 3)
    spread_group(1)
    spread_group(2)
    yleft(0, 2)
    ystart(0, 4)
    loads[7].wait()
    opp_buf[...] = packed(t_opp, grad_v[1])[1]
    ystart(1, 0)
    recv_buf[3, pl.ds(q, 1)] = opp_buf[pl.ds(q, 1)]
    spread_group(3)
    spread_group(4)
    yleft(0, 3)
    ystart(1, 1)
    ystart(1, 2)
    for i in (3, 4, 5):
        loads[i].wait()
    forward(0, 2 * slots)
    opening, closing = unpack_matrices(cap, pieces + 1, n_exp)
    unpack[...] = opening.astype(BF16)
    spread_group(5)
    spread_group(6)
    forward(2 * slots, 4 * slots)
    spread_group(7)
    hand_on(0)
    hand_on(1)
    pack[...] = closing.astype(BF16)
    xt[...] = xb[...].T
    loads[6].wait()

    lane_q = iota((slots, LANES), 1) == q
    blank = 128 - slots

    def rows_of(tt):
        return pl.ds(pl.multiple_of(tt * slots, 32), slots)

    rows_z = d // n_dp
    hops = n_dp // 2

    fold = rows_z // 2
    first_lanes = iota((fold, 128), 1) < rest

    def zslot(way, sub, s):
        return zrest.at[way, s] if sub == 3 else zbuf.at[way, sub, s]

    def zstart(sub):
        return zfirst_r if sub == 3 else zfirst.at[sub]

    def zcopy(way, sub, s, src):
        return remote(
            src, zslot(way, sub, s), zsend.at[way, sub, s], zrecv.at[way, sub, s], "dp", g_left if way else g_right
        )

    def zrows(way, s):
        owner = (g + hops + s) % n_dp if way else (g + n_dp + hops - s) % n_dp
        return pl.ds(pl.multiple_of(owner * rows_z, 16), rows_z)

    def term(sub, chunks):
        def left(ref):
            return jnp.concatenate([ref[rows, :] for rows in chunks], axis=0)

        if sub < 3:
            right = (gate_g, up_g, hid_r)[sub]
            both = dot(left(st if sub == 2 else xt), right[:, :LANES])
            return [both[rows_z * i : rows_z * (i + 1), :] for i in range(len(chunks))]
        wide_part, narrow = dot(left(xt), gate_up[...]), dot(left(st), hid_rest[...])
        parts = []
        for i in range(len(chunks)):
            at = rows_z * i
            folded = jnp.where(first_lanes, narrow[at : at + fold, :], narrow[at + fold : at + rows_z, :])
            pad = jnp.zeros((zfirst_r.shape[0] - rows_z - fold, 128), F32)
            parts.append(jnp.concatenate([wide_part[at : at + rows_z, :], folded, pad], axis=0))
        return parts

    def zpiece(s, sub):
        terms = term(sub, [zrows(0, s), zrows(1, s)])
        for way in range(2):
            total = terms[way]
            slot = zslot(way, sub, s - 1)
            zcopy(way, sub, s - 1, slot).wait_recv()
            slot[...] = (total + slot[...].astype(F32)).astype(BF16)
            zcopy(way, sub, s, slot).start()

    def zsteps(first, end):
        def step(s, carry):
            for sub in range(4):
                zpiece(s, sub)
                if first > 2:
                    for way in range(2):
                        zcopy(way, sub, s - 2, zslot(way, sub, s - 2)).wait_send()
            return carry

        lax.fori_loop(first, end, step, 0)

    def zfirst_pair(sub):
        way = sub % 2
        begin, later = term(sub, [zrows(way, 0), zrows(1 - way, 1)])
        zstart(sub)[...] = begin.astype(BF16)
        zcopy(way, sub, 0, zstart(sub)).start()
        slot = zslot(1 - way, sub, 0)
        slot[...] = later.astype(BF16)
        zcopy(1 - way, sub, 1, slot).start()

    def zsecond(sub):
        way = sub % 2
        slot = zslot(way, sub, 0)
        total = term(sub, [zrows(way, 1)])[0]
        zcopy(way, sub, 0, slot).wait_recv()
        slot[...] = (total + slot[...].astype(F32)).astype(BF16)
        zcopy(way, sub, 1, slot).start()

    def opened_block(rel, tt):
        rows = rows_of(tt)
        opened = dot(unpack[...], recv_buf[rel].reshape(n_exp * CHUNK, LANES))

        def piece(j):
            return opened[slots * j : slots * (j + 1), :]

        weight = jnp.sum(jnp.where(lane_q, piece(pieces), 0.0), axis=1, keepdims=True)
        dy = jnp.concatenate([piece(j) for j in range(pieces)], axis=1)
        at = slice(128 * rel, 128 * (rel + 1))
        st[:, at] = jnp.concatenate([(weight * dy).astype(BF16), jnp.zeros((blank, d), BF16)], axis=0).T
        hid_r[at, :] = jnp.concatenate([hid_s[rows, :], jnp.zeros((blank, hid), BF16)], axis=0)

        def hidden_part():
            finish_block(rows, dy.astype(BF16), weight)

        return hidden_part

    def finish_block(rows, dy, weight):
        back = dot(dy, wd[...], nt)
        prob = jnp.sum(hid_s[rows, :].astype(F32) * back, axis=1, keepdims=True)
        prob_s[rows, :] = jnp.broadcast_to(prob, (slots, 128))
        hidden_grad = weight * back
        gate_g[rows, :] = (hidden_grad * slope_up[rows, :]).astype(BF16)
        up_g[rows, :] = (hidden_grad * silu_s[rows, :]).astype(BF16)

    def backward(rel, tt):
        opened_block(rel, tt)()

    backward(0, t)
    hand_on(2)
    hand_on(3)
    for i in range(6):
        xcopy(0, i).wait_recv()
    backward(1, t_left)
    for i in (0, 1, 2, 3, 4, 6):
        xcopy(1, i).wait_recv()
    backward(2, t_right)
    for away in extra:
        for i in at_distance(away):
            ywait(1, i)
    for i in range(4):
        hand(i).wait_recv()
    hidden_part = opened_block(3, t_opp)
    zfirst_pair(2)
    hidden_part()
    gate_up[...] = jnp.concatenate([gate_g[:, LANES:], up_g[:, LANES:]], axis=1)
    hid_rest[...] = jnp.concatenate([hid_r[:, LANES:], hid_r[:, LANES:]], axis=1)

    def input_part(tt):
        rows = rows_of(tt)
        return dot(gate_g[rows, :], wg[...]) + dot(up_g[rows, :], wu[...])

    def put_part(ref, tt):
        ref[:, :d] = input_part(tt).astype(BF16)
        ref[:, d:] = prob_s[rows_of(tt), :].astype(BF16)

    lo, hi = pl.ds(0, half), pl.ds(half, half)
    first_right = remote(xs_opp.at[lo], xr1.at[0], rsend.at[0], rrecv.at[0], "tensor", t_right)
    first_left = remote(xs_opp.at[hi], xr1.at[1], rsend.at[1], rrecv.at[1], "tensor", t_left)
    plain_right = remote(xs_right.at[hi], xr2.at[0, hi], rsend.at[2], rrecv.at[2], "tensor", t_right)
    plain_left = remote(xs_left.at[lo], xr2.at[1, lo], rsend.at[3], rrecv.at[3], "tensor", t_left)
    added_right = remote(xs_right.at[lo], xr2.at[0, lo], rsend.at[4], rrecv.at[4], "tensor", t_right)
    added_left = remote(xs_left.at[hi], xr2.at[1, hi], rsend.at[5], rrecv.at[5], "tensor", t_left)

    for sub in (1, 0, 3):
        zfirst_pair(sub)
    put_part(xs_opp, t_opp)
    first_right.start()
    first_left.start()

    for sub in (2, 1, 0, 3):
        zsecond(sub)
    put_part(xs_right, t_right)
    plain_right.start()
    put_part(xs_left, t_left)
    plain_left.start()
    zsteps(2, 3)
    first_right.wait_recv()
    xs_right[lo, :] = (xs_right[lo, :].astype(F32) + xr1[0].astype(F32)).astype(BF16)
    added_right.start()
    first_left.wait_recv()
    xs_left[hi, :] = (xs_left[hi, :].astype(F32) + xr1[1].astype(F32)).astype(BF16)
    added_left.start()
    own_part[...] = input_part(t)

    zsteps(3, 4)
    for copy in (plain_right, plain_left, added_right, added_left):
        copy.wait_recv()
    slot_input = own_part[...] + xr2[0, :, :d].astype(F32) + xr2[1, :, :d].astype(F32)
    slot_prob = prob_s[rows_of(t), :] + xr2[0, :, d:].astype(F32) + xr2[1, :, d:].astype(F32)
    slot_prob = jnp.where(lane_q, jnp.concatenate([slot_prob] * (LANES // 128), axis=1), 0.0)
    pile = jnp.concatenate(
        [slot_input[:, LANES * j : LANES * (j + 1)] for j in range(pieces)] + [slot_prob], axis=0
    ).astype(BF16)
    ret_send[...] = dot(pack[...], pile).astype(BF16).reshape(n_exp, CHUNK, LANES)

    def partner(i):
        step = i // 2 + 1
        return (q + (i % 2) * (n_exp - 2 * step) + step) % n_exp

    def wcopy(i):
        p = partner(i)
        return remote(ret_send.at[p], ret_recv.at[q], wsend.at[p], wrecv.at[q], "expert", p)

    def wstart(i, carry):
        wcopy(i).start()
        return carry

    lax.fori_loop(0, n_exp - 1, wstart, 0)
    ret_recv[pl.ds(q, 1)] = ret_send[pl.ds(q, 1)]

    zsteps(4, 6)

    def wwait(i, carry):
        p = partner(i)
        remote(ret_send.at[p], ret_recv.at[p], wsend.at[p], wrecv.at[p], "expert", p).wait_recv()
        return carry

    lax.fori_loop(0, n_exp - 1, wwait, 0)
    tokens = dot(place_t[...], ret_recv[...].reshape(n_exp * CHUNK, LANES))
    for j in range(pieces):
        gather[0, :, LANES * j : LANES * (j + 1)] = tokens[share * j : share * (j + 1), :].astype(BF16)
    prob_pos = tokens[share * pieces :, :128]
    prob_tk = jnp.zeros((share, 128), F32)
    ids = ids_s[tokens_of(t), :]
    for k in range(top):
        val = jnp.sum(jnp.where(ids[:, k : k + 1] == name, prob_pos, 0.0), axis=1, keepdims=True)
        prob_tk = jnp.where(lane == k, val, prob_tk)
    gather[0, :, d:] = prob_tk.astype(BF16)

    low, high = pl.ds(0, share // 2), pl.ds(share // 2, share // 2)
    to_right = remote(gather.at[0], gather.at[1], gsend.at[0], grecv.at[0], "tensor", t_right)
    to_left = remote(gather.at[0], gather.at[2], gsend.at[1], grecv.at[1], "tensor", t_left)
    on_right = remote(gather.at[1, low], gather.at[3, low], gsend.at[2], grecv.at[2], "tensor", t_right)
    on_left = remote(gather.at[2, high], gather.at[3, high], gsend.at[3], grecv.at[3], "tensor", t_left)
    to_right.start()
    to_left.start()

    def sent(i, carry):
        wcopy(i).wait_send()
        return carry

    lax.fori_loop(0, n_exp - 1, sent, 0)
    for away in (0, 4):
        yleft(0, away)
    for away in extra:
        yleft(1, away)
    for i in range(groups):
        xcopy(0, i).wait_send()
        xcopy(1, i).wait_send()
    for i in range(4):
        hand(i).wait_send()
    for copy in (first_right, first_left, plain_right, plain_left, added_right, added_left):
        copy.wait_send()
    for sub in range(4):
        zcopy(sub % 2, sub, 0, zstart(sub)).wait_send()

    def put_tokens(rel, tt):
        rows = pl.ds(pl.multiple_of(tt * share, share), share)
        out_ref[rows, :] = gather[rel, :, :d]
        prob_all[rows, :] = gather[rel, :, d:].astype(F32)

    put_tokens(0, t)
    zsteps(6, 7)
    to_right.wait_recv()
    on_right.start()
    to_left.wait_recv()
    on_left.start()
    put_tokens(1, t_left)
    put_tokens(2, t_right)
    zsteps(7, hops)
    on_right.wait_recv()
    on_left.wait_recv()
    put_tokens(3, t_opp)

    own = []
    for sub in range(4):
        total = term(sub, [zrows(0, hops)])[0]
        for way in range(2):
            slot = zslot(way, sub, hops - 1)
            zcopy(way, sub, hops - 1, slot).wait_recv()
            total = total + slot[...].astype(F32)
        own.append(total)
    folded = own[3][rows_z : rows_z + fold, :]
    own[3:] = [own[3][:rows_z, :], jnp.concatenate([folded, pltpu.roll(folded, 128 - rest, 1)], axis=0)]
    own = [jnp.concatenate([o, jnp.zeros((128 - rows_z, o.shape[1]), F32)], axis=0).T[:, :rows_z] for o in own]
    gate_out[:LANES, :] = own[0]
    gate_out[LANES:, :] = own[3][:rest]
    up_out[:LANES, :] = own[1]
    up_out[LANES:, :] = own[3][rest : 2 * rest]
    down_out[:LANES, :] = own[2]
    down_out[LANES:, :] = own[4][:rest]
    prob_out[...] = prob_all[...].T[:top]

    for copy in (to_right, to_left, on_right, on_left):
        copy.wait_send()


    def zsent(s, carry):
        for way in range(2):
            for sub in range(4):
                zcopy(way, sub, s, zslot(way, sub, s)).wait_send()
        return carry

    lax.fori_loop(hops - 2, hops, zsent, 0)


def finish(*refs):
    for src, dst in zip(refs[:5], refs[5:]):
        dst[...] = src[...]


def shards(grad_out, expert_ids, gate_probs, saved_inputs, w_gate, w_up, w_down):
    n_dp, n_exp, n_ten = lax.axis_size("dp"), lax.axis_size("expert"), lax.axis_size("tensor")
    tok_rows, d = grad_out.shape
    cap, top, hid = saved_inputs.shape[4], expert_ids.shape[1], w_gate.shape[2]
    share = tok_rows // n_ten
    slots = n_exp * cap
    total = n_ten * slots
    wide = d + 128
    rows_z = d // n_dp
    rest_rows = rows_z + -(-rows_z // 2 // 16) * 16
    vmem = pltpu.VMEM
    dma = pltpu.SemaphoreType.DMA
    shapes = (
        jax.ShapeDtypeStruct((tok_rows, d), BF16),
        jax.ShapeDtypeStruct((top, tok_rows), F32),
        jax.ShapeDtypeStruct((hid, rows_z), F32),
        jax.ShapeDtypeStruct((hid, rows_z), F32),
        jax.ShapeDtypeStruct((hid, rows_z), F32),
    )
    outs = pl.pallas_call(
        lambda *refs: kernel((n_dp, n_exp, n_ten, cap, top, d, hid), *refs),
        out_shape=shapes,
        in_specs=[pl.BlockSpec(memory_space=pl.ANY)] * 7,
        out_specs=(pl.BlockSpec(memory_space=pltpu.VMEM),) * 5,
        scratch_shapes=[
            vmem((2, share, d), BF16),
            vmem((top, tok_rows), jnp.int32),
            vmem((top, tok_rows), F32),
            vmem((total, d), BF16),
            vmem((hid, d), BF16),
            vmem((hid, d), BF16),
            vmem((hid, d), BF16),
            vmem((tok_rows, 128), F32),
            vmem((tok_rows, 128), F32),
            vmem((tok_rows, 128), F32),
            vmem((n_exp * CHUNK, n_exp * CHUNK), BF16),
            vmem((n_exp * CHUNK, n_exp * CHUNK), BF16),
            vmem((n_exp, CHUNK, LANES), BF16),
            vmem((n_exp, CHUNK, LANES), BF16),
            vmem((4, n_exp, CHUNK, LANES), BF16),
            vmem((LANES, n_exp * CHUNK), BF16),
            vmem((d, total), BF16),
            vmem((d, 4 * 128), BF16),
            vmem((total, hid), F32),
            vmem((total, hid), F32),
            vmem((total, hid), BF16),
            vmem((4 * 128, hid), BF16),
            vmem((total, hid), BF16),
            vmem((total, hid), BF16),
            vmem((total, 128), BF16),
            vmem((4 * 128, 128), BF16),
            vmem((total, 128), F32),
            vmem((slots, d), F32),
            vmem((slots, wide), BF16),
            vmem((slots, wide), BF16),
            vmem((slots, wide), BF16),
            vmem((2, slots // 2, wide), BF16),
            vmem((2, slots, wide), BF16),
            vmem((n_exp, CHUNK, LANES), BF16),
            vmem((n_exp, CHUNK, LANES), BF16),
            vmem((4, share, wide), BF16),
            vmem((3, rows_z, LANES), BF16),
            vmem((rest_rows, 128), BF16),
            vmem((2, 3, n_dp // 2, rows_z, LANES), BF16),
            vmem((2, n_dp // 2, rest_rows, 128), BF16),
            dma((8,)),
            dma((2, n_exp)),
            dma((2, n_exp)),
            dma((3, n_exp // 2)),
            dma((3, n_exp // 2)),
            dma((6,)),
            dma((6,)),
            dma((n_exp,)),
            dma((n_exp,)),
            dma((4,)),
            dma((4,)),
            dma((2, 4, n_dp // 2)),
            dma((2, 4, n_dp // 2)),
        ],
        compiler_params=pltpu.CompilerParams(
            collective_id=0, has_side_effects=True, vmem_limit_bytes=56 * 1024 * 1024
        ),
        name="expert_backward",
    )(
        grad_out,
        expert_ids.T,
        gate_probs.T,
        saved_inputs.transpose(0, 1, 2, 4, 3, 5).reshape(total, d),
        w_gate[0].T,
        w_up[0].T,
        w_down[0].T,
    )
    outs = pl.pallas_call(
        finish,
        out_shape=shapes,
        in_specs=[pl.BlockSpec(memory_space=pltpu.VMEM)] * 5,
        out_specs=(pl.BlockSpec(memory_space=pltpu.VMEM),) * 5,
        name="write_results",
    )(*outs)
    return outs[0], outs[1].T, outs[2].T[None], outs[3].T[None], outs[4].T[None]


def solution(mesh):
    return jax.shard_map(
        shards,
        mesh=mesh,
        in_specs=(
            P(("dp", "expert"), None),
            P(("dp", "expert"), None),
            P(("dp", "expert"), None),
            P("dp", "expert", None, None, None, None),
            P("expert", None, "tensor"),
            P("expert", None, "tensor"),
            P("expert", None, "tensor"),
        ),
        out_specs=(
            P(("dp", "expert"), None),
            P(("dp", "expert"), None),
            P("expert", "dp", "tensor"),
            P("expert", "dp", "tensor"),
            P("expert", "dp", "tensor"),
        ),
        check_vma=False,
    )
```
